256 devices in a mesh: band: 8 (over x, core), freq: 32 (over z, y).
Axes of the slice: x: 4, y: 4, z: 8, core: 2. Of those that a mesh axis runs over, the one named last changes fastest.
Arguments:
- samples: float32 [4096, 16384], P('band', 'freq'), may hold values from -6 to 6
- channel_delay: int32 [4096, 64], P('band'), may hold values from 0 to 4095
- merge_slope: int32 [15], replicated, may hold values from 16 to 1023
- tap_offset: int32 [32, 16], replicated, may hold values from -32 to 32, as said below
- tap_weight: float32 [32, 16], replicated, may hold values from -1.5 to 1.5
Outputs:
- best_power: float32 [1024, 8192], P('band', 'freq')
The draws below stay inside these ranges and needn't reach their ends.
Inputs may be any that keep to these rules, and one draw needn't show every extreme that they name: `tap_offset`: in every draw some template has a tap at offset -32 and some template has one at 32.
All inputs are finite; a program needn't handle non-finite values.
Results may differ from the reference program's by a relative error of at most 0.0003.
Values sent between devices are 32-bit elements; how exact they have to be, the bound alone decides.
No kernel may reach another device: no remote copies, remote signals or barrier semaphores. Data moves between devices by JAX's collectives and lax.ppermute only.
A program may use at most 128 MiB of HBM per device.

```python
import math
import jax
import jax.numpy as jnp
import numpy as np
from jax import lax

CH_SUB = 256
SAMPLES = 16384
SUB_DELAYS = 64
TEMPLATES = 32
TAPS = 16
REACH = 32
SUBBANDS = 16
CHANNELS = 4096
HALF = 8192
FINAL = 1024


def draw_tap_offset(key, part):
    key_table = jax.random.fold_in(key, 11)
    key_pick = jax.random.fold_in(key, 12)
    offsets_table = jax.random.randint(key_table, (TEMPLATES, TAPS), -REACH, REACH + 1)
    chosen = jax.random.randint(key_pick, (2,), 0, TEMPLATES)
    offsets_table = offsets_table.at[chosen[0], 0].set(-REACH)
    offsets_table = offsets_table.at[chosen[1], 1].set(REACH)
    return offsets_table.astype(jnp.int32)


def set_ends(values, own_key, smallest, top_value):
    place = [jax.random.randint(jax.random.fold_in(own_key, axis), (), 0, length) for axis, length in enumerate(values.shape)]
    longest = values.shape.index(max(values.shape))
    next_to = place[:longest] + [(place[longest] + 1) % values.shape[longest]] + place[longest + 1:]
    return values.at[tuple(place)].set(smallest).at[tuple(next_to)].set(top_value)


def block_scale(own_key, dims, pieces, low, top_value):
    factor_of, own = 1.0, jax.random.fold_in(own_key, 6)
    for axis_at, shards_of in pieces:
        steps = jnp.exp(jax.random.uniform(jax.random.fold_in(own, axis_at), (shards_of,), jnp.float32, low / len(pieces), top_value / len(pieces)))
        factor_of = factor_of * jnp.repeat(steps, dims[axis_at] // shards_of).reshape([-1 if axis == axis_at else 1 for axis in range(len(dims))])
    return factor_of


def centred(key, dims, scale, reach, shards=(), held_as=jnp.bfloat16):
    factor_of = block_scale(key, dims, shards, -0.22, 0.18) if shards else 1.0
    drawn = jax.random.normal(key, dims, jnp.float32) * scale * factor_of
    return jnp.minimum(jnp.maximum(drawn, -reach), reach).astype(held_as)


def setup_inputs(seed: int = 0) -> dict:
    keys = jax.random.split(jax.random.key(seed), 6)
    samples = centred(keys[0], (CHANNELS, SAMPLES), 1.0, 6.0, ((0, 8), (1, 32)), jnp.float32)
    channel_delay = set_ends(jax.random.randint(keys[1], (CHANNELS, SUB_DELAYS), 0, 4096), jax.random.fold_in(keys[1], 1), 0, 4095).astype(jnp.int32)
    merge_slope = set_ends(jax.random.randint(keys[2], (SUBBANDS - 1,), 16, 1024), jax.random.fold_in(keys[2], 1), 16, 1023).astype(jnp.int32)
    tap_offset = draw_tap_offset(jax.random.fold_in(keys[5], 71), 0)
    tap_weight = centred(keys[4], (TEMPLATES, TAPS), TAPS ** -0.5, 1.5, (), jnp.float32)
    return {"samples": samples, "channel_delay": channel_delay, "merge_slope": merge_slope, "tap_offset": tap_offset, "tap_weight": tap_weight}


two_pi = 2.0 * math.pi

def turning(count, modulus):
    angle = (count % modulus).astype(jnp.float32) * (two_pi / modulus)
    return (jnp.cos(angle), jnp.sin(angle))

def rotate(real, imag, cosine, sine_part):
    return (real * cosine + imag * sine_part, imag * cosine - real * sine_part)

def merge_nodes(lower_half, upper_half, out_index, slopes, bins_index, modulus):
    shift = out_index[None, :] * slopes[:, None] // 16 % modulus
    cosine, sine_part = turning(shift[:, :, None] * bins_index[None, None, :], modulus)
    up_re, up_im = rotate(upper_half[0], upper_half[1], cosine, sine_part)
    return jnp.stack([lower_half[0] + up_re, lower_half[1] + up_im]) * (1.0 / math.sqrt(2.0))

def reference(samples, channel_delay, merge_slope, tap_offset, tap_weight):
    spectrum = jnp.fft.rfft(samples, axis=1)[:, :HALF] / math.sqrt(SAMPLES)
    spec_re = jnp.real(spectrum).astype(jnp.float32)
    spec_im = jnp.imag(spectrum).astype(jnp.float32)
    fine_bins = lax.iota(jnp.int32, 128)
    coarse_bins = lax.iota(jnp.int32, HALF // 128) * 128

    def one_subband(inputs):
        band_re, band_im, band_delay = inputs
        delay_blocks = band_delay.reshape(CH_SUB, SUB_DELAYS // 8, 8).transpose(1, 0, 2)

        def one_block(delay_cols):
            coarse_cos, coarse_sin = turning(delay_cols[:, :, None] * coarse_bins[None, None, :], SAMPLES)
            fine_cos, fine_sin = turning(delay_cols[:, :, None] * fine_bins[None, None, :], SAMPLES)
            full_cos = coarse_cos[..., None] * fine_cos[..., None, :] - coarse_sin[..., None] * fine_sin[..., None, :]
            full_sin = coarse_sin[..., None] * fine_cos[..., None, :] + coarse_cos[..., None] * fine_sin[..., None, :]
            full_cos = full_cos.reshape(CH_SUB, 8, HALF)
            full_sin = full_sin.reshape(CH_SUB, 8, HALF)
            turned_re, turned_im = rotate(band_re[:, None, :], band_im[:, None, :], full_cos, full_sin)
            return (lax.optimization_barrier(jnp.sum(turned_re, axis=0)), lax.optimization_barrier(jnp.sum(turned_im, axis=0)))
        sums_re, sums_im = lax.map(one_block, delay_blocks)
        return (sums_re.reshape(SUB_DELAYS, HALF), sums_im.reshape(SUB_DELAYS, HALF))
    sub_re, sub_im = lax.map(one_subband, (spec_re.reshape(SUBBANDS, CH_SUB, HALF), spec_im.reshape(SUBBANDS, CH_SUB, HALF), channel_delay.reshape(SUBBANDS, CH_SUB, SUB_DELAYS)))
    current = jnp.stack([sub_re, sub_im]) * (1.0 / math.sqrt(CH_SUB))
    bins_index = lax.iota(jnp.int32, HALF)
    section_count = SUBBANDS.bit_length() - 1
    for section_no in range(section_count):
        d_in = current.shape[2]
        lower_half = current[:, 0::2]
        upper_half = current[:, 1::2]
        lower_half = jnp.concatenate([lower_half, lower_half], axis=2)
        upper_half = jnp.concatenate([upper_half, upper_half], axis=2)
        node_count = lower_half.shape[1]
        slope_rows = merge_slope[np.array([node_no * (2 << section_no) + (1 << section_no) - 1 for node_no in range(node_count)], dtype=np.int32)]
        current = merge_nodes(lower_half, upper_half, lax.iota(jnp.int32, 2 * d_in), slope_rows, bins_index, SAMPLES)
    padded_re = jnp.pad(current[0, 0], ((0, 0), (REACH, REACH)))
    padded_im = jnp.pad(current[1, 0], ((0, 0), (REACH, REACH)))

    def one_template(template_no, best):

        def one_tap(tap_no, totals):
            start = (tap_offset[template_no, tap_no] + REACH).astype(jnp.int32)
            weight = tap_weight[template_no, tap_no]
            return (totals[0] + weight * lax.dynamic_slice_in_dim(padded_re, start, HALF, 1), totals[1] + weight * lax.dynamic_slice_in_dim(padded_im, start, HALF, 1))
        zeros_grid = jnp.zeros((FINAL, HALF), jnp.float32)
        corr_re, corr_im = lax.fori_loop(0, TAPS, one_tap, (zeros_grid, zeros_grid))
        return jnp.maximum(best, corr_re * corr_re + corr_im * corr_im)
    return lax.fori_loop(0, TEMPLATES, one_template, jnp.zeros((FINAL, HALF), jnp.float32))
```

```python
import math

import jax
import jax.numpy as jnp
import numpy as np
from jax import lax
from jax.experimental import pallas as pl
from jax.experimental.pallas import tpu as pltpu
from jax.sharding import PartitionSpec as P

REACH = 32
LANES = 128
ROOT = 64
D_BLOCK = 32

two_pi = 2.0 * math.pi
top_precision = lax.Precision.HIGHEST
f32 = jnp.float32
bf16 = jnp.bfloat16


def turning(count, modulus):
    angle = (count % modulus).astype(f32) * (two_pi / modulus)
    return (jnp.cos(angle), jnp.sin(angle))


def rotate(real, imag, cosine, sine_part):
    return (real * cosine + imag * sine_part, imag * cosine - real * sine_part)


def pick_entry(table, index):
    return jnp.sum(jnp.where(lax.iota(jnp.int32, table.shape[0]) == index, table, 0))


def split_bf16(value):
    high = value.astype(bf16)
    return high, (value - high.astype(f32)).astype(bf16)


def transform(blocks, length):
    sources, rows, samp = blocks.shape
    inner = length // LANES
    grid = blocks.transpose(1, 0, 2).reshape(rows, inner, LANES)
    index = lax.iota(jnp.int32, LANES)
    cos_first, sin_first = turning(index[:, None] * index[None, :], inner)
    part_re = jnp.einsum("cab,ak->ckb", grid, cos_first, precision=top_precision)
    part_im = -jnp.einsum("cab,ak->ckb", grid, sin_first, precision=top_precision)
    cos_twist, sin_twist = turning(index[:, None] * index[None, :], length)
    part_re, part_im = rotate(part_re, part_im, cos_twist, sin_twist)
    column = lax.iota(jnp.int32, LANES)
    kept = column // 4 * 2 + column % 2
    imag_col = (column // 2 % 2 == 1)[None, :]
    cos_second, sin_second = turning(index[:, None] * kept[None, :], LANES)
    scale = 1.0 / math.sqrt(length) / 16.0 / 4.0
    from_re = jnp.where(imag_col, -sin_second, cos_second) * scale
    from_im = jnp.where(imag_col, cos_second, sin_second) * scale
    both = jnp.concatenate([part_re, part_im], axis=2)
    out = jnp.einsum(
        "ckb,bm->cmk", both, jnp.concatenate([from_re, from_im], axis=0), precision=top_precision
    )
    slabs = LANES // 4
    return out.reshape(rows, slabs, 4, LANES).transpose(1, 0, 2, 3).reshape(slabs, rows * 4, LANES)


def base_tiles(first_bin, length):
    row = np.arange(4 * ROOT * 8)
    kind, step, sub_row = row // (ROOT * 8), row % (ROOT * 8) // 8, row % 8
    q = length // 4
    turns = np.array([[0, 3 * q, q, 0], [q, 0, 2 * q, q], [0] * 4, [3 * q] * 4])
    offset = turns[kind, sub_row // 2].astype(np.int32)
    shift = np.where(kind < 2, ROOT * step, step).astype(np.int32)
    half = (sub_row % 2 * LANES).astype(np.int32)
    bins = first_bin + half[:, None] + lax.iota(jnp.int32, LANES)[None, :]
    return turning(bins * shift[:, None] + offset[:, None], length)[0]


def sub_kernel(delay_ref, spec_ref, base_ref, tw_ref, out_ref, table, sums):
    group = 8

    def fill(block, carry):
        first = [base_ref[pl.ds((block * group + i) * 8, 8), :] for i in range(group)]
        second = [base_ref[pl.ds((ROOT + block * group + i) * 8, 8), :] for i in range(group)]

        def inner(q, c):
            cos_q = base_ref[pl.ds((2 * ROOT + q) * 8, 8), :]
            sin_q = base_ref[pl.ds((3 * ROOT + q) * 8, 8), :]
            for i in range(group):
                table[(block * group + i) * ROOT + q] = first[i] * cos_q + second[i] * sin_q
            return c

        return lax.fori_loop(0, ROOT, inner, carry, unroll=4)

    lax.fori_loop(0, ROOT // group, fill, 0)

    channels = spec_ref.shape[0] // 4
    per_sub = channels // 2
    delays = delay_ref.shape[0] // channels
    low_rows = lax.broadcasted_iota(jnp.int32, (8, LANES), 0) < 4
    for sb in range(2):
        for db in range(delays // D_BLOCK):

            def body(pair, accs):
                accs = list(accs)
                chan = sb * per_sub + 2 * pair
                tile = spec_ref[pl.ds(pl.multiple_of(chan * 4, 8), 8), :]
                turned = pltpu.roll(tile, 4, 0)
                start = chan * delays + db * D_BLOCK
                for j, mine in enumerate(
                    (jnp.where(low_rows, tile, turned), jnp.where(low_rows, turned, tile))
                ):
                    for d in range(D_BLOCK):
                        accs[d] = accs[d] + mine * table[delay_ref[start + j * delays + d]]
                return tuple(accs)

            zero = jnp.zeros((8, LANES), f32)
            accs = lax.fori_loop(0, per_sub // 2, body, (zero,) * D_BLOCK)
            for d in range(D_BLOCK):
                whole = accs[d] + pltpu.roll(accs[d], 6, 0)
                at = sb * delays + db * D_BLOCK + d
                sums[0, at : at + 1, 0:LANES] = whole[0:1]
                sums[0, at : at + 1, LANES:] = whole[1:2]
                sums[1, at : at + 1, 0:LANES] = whole[4:5]
                sums[1, at : at + 1, LANES:] = whole[5:6]

    re = sums[0].T
    im = sums[1].T
    re_turn = pltpu.roll(re, delays, 1)
    im_turn = pltpu.roll(im, delays, 1)
    left = lax.broadcasted_iota(jnp.int32, re.shape, 1) < delays
    up_re, up_im = rotate(
        jnp.where(left, re_turn, re), jnp.where(left, im_turn, im), tw_ref[0], tw_ref[1]
    )
    out_ref[0] = jnp.where(left, re, re_turn) + up_re
    out_ref[1] = jnp.where(left, im, im_turn) + up_im


def toeplitz_kernel(profile_ref, high_ref, low_ref):
    def body(a, carry):
        row = profile_ref[pl.ds(a, 1), :]
        wide = jnp.broadcast_to(row, (LANES, row.shape[1]))
        band = pltpu.roll(wide, 0, 1, stride=1, stride_axis=0)
        high, low = split_bf16(band)
        at = pl.ds(pl.multiple_of(a * LANES, LANES), LANES)
        high_ref[at, :] = high
        low_ref[at, :] = low
        return carry

    lax.fori_loop(0, profile_ref.shape[0], body, 0)


def corr_kernel(left_ref, mid_ref, right_ref, high_ref, low_ref, out_ref, ext):
    bins = mid_ref.shape[1]
    for x in range(2):
        cols = slice(x * LANES, (x + 1) * LANES)
        ext[0:REACH, cols] = left_ref[x]
        ext[REACH : REACH + bins, cols] = mid_ref[x]
        ext[REACH + bins : bins + 2 * REACH, cols] = right_ref[x]
        ext[bins + 2 * REACH :, cols] = jnp.zeros((ext.shape[0] - bins - 2 * REACH, LANES), f32)
    per = 4
    templates = high_ref.shape[0] // LANES
    for kb in range(bins // LANES):
        win_high, win_low = split_bf16(ext[kb * LANES : kb * LANES + 2 * LANES, :])

        def body(step, best):
            at = pl.ds(pl.multiple_of(step * per * LANES, LANES), per * LANES)
            high = high_ref[at, :]
            low = low_ref[at, :]
            got = (
                jnp.dot(high, win_high, preferred_element_type=f32)
                + jnp.dot(high, win_low, preferred_element_type=f32)
                + jnp.dot(low, win_high, preferred_element_type=f32)
            )
            for i in range(per):
                re = got[i * LANES : (i + 1) * LANES, :LANES]
                im = got[i * LANES : (i + 1) * LANES, LANES:]
                best = jnp.maximum(best, re * re + im * im)
            return best

        best = lax.fori_loop(0, templates // per, body, jnp.zeros((LANES, LANES), f32))
        out_ref[:, kb * LANES : (kb + 1) * LANES] = best.T


def per_device(samples, channel_delay, merge_slope, tap_offset, tap_weight):
    freq_count = lax.axis_size("freq")
    band_count = lax.axis_size("band")
    band_pos = lax.axis_index("band")
    freq_pos = lax.axis_index("freq")
    chan_dev, samp_dev = samples.shape
    length = samp_dev * freq_count
    bins_dev = length // 2 // freq_count
    delays_sub = channel_delay.shape[1]
    block = 2 * delays_sub
    vmem = pl.BlockSpec(memory_space=pltpu.VMEM)
    smem = pl.BlockSpec(memory_space=pltpu.SMEM)

    first_bin = freq_pos * bins_dev
    base = base_tiles(first_bin, length)
    bins_index = first_bin + lax.iota(jnp.int32, bins_dev)
    sections = band_count.bit_length()
    shifts = []
    for s in range(sections):
        size = 1 << s
        slope = pick_entry(merge_slope, band_pos // size * (2 * size) + size - 1)
        out_index = band_pos % size * block + lax.iota(jnp.int32, block)
        shifts.append(out_index * slope // 16 % length)
    turn_cos, turn_sin = turning(
        jnp.stack(shifts)[:, None, :] * bins_index[None, :, None], length
    )
    turns = jnp.stack([turn_cos, turn_sin], axis=1)
    window = 2 * LANES
    matches = tap_offset[:, :, None] + REACH == lax.iota(jnp.int32, window)[None, None, :]
    profile = jnp.sum(jnp.where(matches, tap_weight[:, :, None], 0.0), axis=1)
    templates = profile.shape[0]
    band_shape = jax.ShapeDtypeStruct((templates * LANES, window), bf16)
    high, low = pl.pallas_call(
        toeplitz_kernel,
        out_shape=(band_shape, band_shape),
        in_specs=[vmem],
        out_specs=(vmem, vmem),
        name="toeplitz",
    )(profile)

    blocks = samples.reshape(freq_count, chan_dev // freq_count, samp_dev)
    blocks = lax.all_to_all(blocks, "freq", split_axis=0, concat_axis=0, tiled=True)
    spec = transform(blocks, length)
    spec = lax.all_to_all(spec, "freq", split_axis=0, concat_axis=0, tiled=True)
    spec = spec.reshape(chan_dev * 4, LANES)

    current = pl.pallas_call(
        sub_kernel,
        out_shape=jax.ShapeDtypeStruct((2, bins_dev, block), f32),
        in_specs=[smem, vmem, vmem, vmem],
        out_specs=vmem,
        scratch_shapes=[
            pltpu.VMEM((ROOT * ROOT, 8, LANES), f32),
            pltpu.VMEM((2, block, bins_dev), f32),
        ],
        compiler_params=pltpu.CompilerParams(vmem_limit_bytes=40 * 2**20),
        name="subband",
    )(channel_delay.reshape(-1), spec, base, turns[0])

    for s in range(1, sections):
        half = 1 << (s - 1)
        partner = lax.ppermute(current, "band", [(i, i ^ half) for i in range(band_count)])
        upper_side = band_pos % (2 * half) >= half
        lower = jnp.where(upper_side, partner, current)
        upper = jnp.where(upper_side, current, partner)
        up_re, up_im = rotate(upper[0], upper[1], turns[s, 0], turns[s, 1])
        current = jnp.stack([lower[0] + up_re, lower[1] + up_im])

    ends = freq_count - 1
    from_left = lax.ppermute(
        current[:, bins_dev - REACH :], "freq", [(i, i + 1) for i in range(ends)]
    )
    from_right = lax.ppermute(current[:, :REACH], "freq", [(i + 1, i) for i in range(ends)])
    return pl.pallas_call(
        corr_kernel,
        out_shape=jax.ShapeDtypeStruct((block, bins_dev), f32),
        in_specs=[vmem] * 5,
        out_specs=vmem,
        scratch_shapes=[pltpu.VMEM((bins_dev + LANES, 2 * LANES), f32)],
        compiler_params=pltpu.CompilerParams(vmem_limit_bytes=40 * 2**20),
        name="templates",
    )(from_left, current, from_right, high, low)


def solution(mesh):
    placed = (P("band", "freq"), P("band", None), P(), P(), P())
    return jax.shard_map(
        per_device, mesh=mesh, in_specs=placed, out_specs=P("band", "freq"), check_vma=False
    )
```

```python
import math

import jax
import jax.numpy as jnp
from jax import lax
from jax.experimental import pallas as pl
from jax.experimental.pallas import tpu as pltpu
from jax.sharding import PartitionSpec as P

REACH = 32
LANES = 128
GROUP = 8

two_pi = 2.0 * math.pi
top_precision = lax.Precision.HIGHEST
f32 = jnp.float32
bf16 = jnp.bfloat16


def turning(count, modulus):
    angle = (count % modulus).astype(f32) * (two_pi / modulus)
    return (jnp.cos(angle), jnp.sin(angle))


def rotate(real, imag, cosine, sine_part):
    return (real * cosine + imag * sine_part, imag * cosine - real * sine_part)


def pick_entry(table, index):
    return jnp.sum(jnp.where(lax.iota(jnp.int32, table.shape[0]) == index, table, 0))


def split_bf16(value):
    high = value.astype(bf16)
    return high, (value - high.astype(f32)).astype(bf16)


def transform(blocks, length):
    sources, rows, samp = blocks.shape
    inner = length // LANES
    grid = blocks.transpose(1, 0, 2).reshape(rows, inner, LANES)
    index = lax.iota(jnp.int32, LANES)
    cos_first, sin_first = turning(index[:, None] * index[None, :], inner)
    part_re = jnp.einsum("cab,ak->ckb", grid, cos_first, precision=top_precision)
    part_im = -jnp.einsum("cab,ak->ckb", grid, sin_first, precision=top_precision)
    cos_twist, sin_twist = turning(index[:, None] * index[None, :], length)
    part_re, part_im = rotate(part_re, part_im, cos_twist, sin_twist)
    column = lax.iota(jnp.int32, LANES)
    kept = column // 4 * 2 + column % 2
    imag_col = (column // 2 % 2 == 1)[None, :]
    cos_second, sin_second = turning(index[:, None] * kept[None, :], LANES)
    scale = 1.0 / math.sqrt(length) / 16.0 / 4.0
    from_re = jnp.where(imag_col, -sin_second, cos_second) * scale
    from_im = jnp.where(imag_col, cos_second, sin_second) * scale
    both = jnp.concatenate([part_re, part_im], axis=2)
    out = jnp.einsum(
        "ckb,bm->mck", both, jnp.concatenate([from_re, from_im], axis=0), precision=top_precision
    )
    return out.reshape(LANES // 4, 4, rows, LANES)


def delay_turns(channel_delay, first_bin, length):
    per_sub = channel_delay.shape[0] // 2
    both = jnp.concatenate([channel_delay[:per_sub], channel_delay[per_sub:]], axis=1)
    halves = [2 * first_bin + GROUP - 1, 2 * GROUP] + [2 * b + 1 for b in range(GROUP // 2)]
    count = both[None] * jnp.stack([jnp.int32(h) for h in halves])[:, None, None]
    return jnp.stack(turning(count, 2 * length), axis=1)


def spreading():
    shape = (LANES // 2 // GROUP, GROUP // 2, 2 * LANES, 2 * LANES)
    i = [lax.broadcasted_iota(jnp.int32, shape, d) for d in range(4)]
    half = LANES // 2
    source = i[0] * GROUP + i[1] * 2 + i[3] // LANES + i[3] % LANES // half * half
    return (i[2] % LANES == source).astype(bf16)


def sub_kernel(spec_ref, tab_ref, spread_ref, tw_ref, out_ref, parts, centre, wide):
    half = LANES // 2
    per_sub = centre.shape[1]
    sources = spec_ref.shape[0] // 2
    rows = spec_ref.shape[2]
    left = lax.broadcasted_iota(jnp.int32, (rows, LANES), 1) < half

    def arrange(g, carry):
        at = pl.ds(pl.multiple_of(rows * g, rows), rows)
        for x in range(2):
            centre[x, at, :] = tab_ref[0, x, at, :]
            to = pl.ds(pl.multiple_of(per_sub * x + rows * g, rows), rows)
            for h in range(2):
                first = spec_ref[g, 2 * x + h]
                second = spec_ref[sources + g, 2 * x + h]
                pair = (
                    jnp.where(left, first, pltpu.roll(second, half, 1)),
                    jnp.where(left, pltpu.roll(first, half, 1), second),
                )
                for o in range(2):
                    high, low = split_bf16(pair[o])
                    parts[2 * h + o, to, 0:LANES] = high
                    parts[2 * h + o, to, LANES:] = low
        return carry

    lax.fori_loop(0, sources, arrange, 0, unroll=2)
    quarter = spread_ref.shape[0]

    def bins(step, carry):
        for n in range(GROUP // 2):
            for r in range(2):
                at = slice(r * per_sub, (r + 1) * per_sub)
                wide[n, at, :] = jnp.dot(
                    parts[step // quarter, at, :],
                    spread_ref[step % quarter, n],
                    preferred_element_type=f32,
                )

        def channels(g, sums):
            re = list(sums[:GROUP])
            im = list(sums[GROUP:])
            at = pl.ds(pl.multiple_of(8 * g, 8), 8)
            at_im = pl.ds(pl.multiple_of(per_sub + 8 * g, 8), 8)
            mid_cos = centre[0, at, :]
            mid_sin = centre[1, at, :]
            for b in range(GROUP // 2):
                off_cos = tab_ref[2 + b, 0, at, :]
                off_sin = tab_ref[2 + b, 1, at, :]
                cc, ss = mid_cos * off_cos, mid_sin * off_sin
                sc, cs = mid_sin * off_cos, mid_cos * off_sin
                for j, cosine, sine in (
                    (GROUP // 2 + b, cc - ss, sc + cs),
                    (GROUP // 2 - 1 - b, cc + ss, sc - cs),
                ):
                    lanes = slice(j % 2 * LANES, j % 2 * LANES + LANES)
                    real = wide[j // 2, at, lanes]
                    imag = wide[j // 2, at_im, lanes]
                    re[j] = re[j] + (real * cosine + imag * sine)
                    im[j] = im[j] + (imag * cosine - real * sine)
            step_cos = tab_ref[1, 0, at, :]
            step_sin = tab_ref[1, 1, at, :]
            centre[0, at, :] = mid_cos * step_cos - mid_sin * step_sin
            centre[1, at, :] = mid_sin * step_cos + mid_cos * step_sin
            return tuple(re) + tuple(im)

        zero = jnp.zeros((8, LANES), f32)
        sums = lax.fori_loop(0, per_sub // 8, channels, (zero,) * (2 * GROUP), unroll=per_sub // 8)
        at = pl.ds(pl.multiple_of(step * GROUP, GROUP), GROUP)
        re, im = (
            jnp.concatenate(
                [jnp.sum(v, axis=0, keepdims=True) for v in sums[x * GROUP : (x + 1) * GROUP]],
                axis=0,
            )
            for x in range(2)
        )
        lower = lax.broadcasted_iota(jnp.int32, re.shape, 1) < half
        re_turn = pltpu.roll(re, half, 1)
        im_turn = pltpu.roll(im, half, 1)
        up_re, up_im = rotate(
            jnp.where(lower, re_turn, re),
            jnp.where(lower, im_turn, im),
            tw_ref[0, at, :],
            tw_ref[1, at, :],
        )
        out_ref[0, at, :] = jnp.where(lower, re, re_turn) + up_re
        out_ref[1, at, :] = jnp.where(lower, im, im_turn) + up_im
        return carry

    lax.fori_loop(0, out_ref.shape[1] // GROUP, bins, 0)


def toeplitz_kernel(profile_ref, high_ref, low_ref, edge_high_ref, edge_low_ref):
    rows = high_ref.shape[0] // profile_ref.shape[0]

    def body(a, carry):
        row = profile_ref[pl.ds(a, 1), :]
        wide = jnp.broadcast_to(row, (rows, row.shape[1]))
        high, low = split_bf16(pltpu.roll(wide, 0, 1, stride=1, stride_axis=0))
        at = pl.ds(pl.multiple_of(a * rows, rows), rows)
        high_ref[at, :] = high
        low_ref[at, :] = low
        at = pl.ds(pl.multiple_of(a * REACH, REACH), REACH)
        edge_high_ref[at, :] = high[:REACH, :LANES]
        edge_low_ref[at, :] = low[:REACH, :LANES]
        return carry

    lax.fori_loop(0, profile_ref.shape[0], body, 0)


def products(high, low, win_high, win_low):
    return (
        jnp.dot(high, win_high, preferred_element_type=f32)
        + jnp.dot(high, win_low, preferred_element_type=f32)
        + jnp.dot(low, win_high, preferred_element_type=f32)
    )


def power(value):
    re, im = value[:, :LANES], value[:, LANES:]
    return re * re + im * im


def inner_kernel(mid_ref, high_ref, low_ref, out_ref):
    rows = out_ref.shape[0]
    per = 2
    win_high, win_low = split_bf16(jnp.concatenate([mid_ref[0], mid_ref[1]], axis=1))

    def body(step, best):
        at = pl.ds(pl.multiple_of(step * per * rows, rows), per * rows)
        got = products(high_ref[at, :], low_ref[at, :], win_high, win_low)
        for i in range(per):
            best = jnp.maximum(best, power(got[i * rows : (i + 1) * rows]))
        return best

    steps = high_ref.shape[0] // (per * rows)
    out_ref[...] = lax.fori_loop(0, steps, body, jnp.zeros(out_ref.shape, f32), unroll=4)


def edge_kernel(left_ref, mid_ref, right_ref, inner_ref, high_ref, low_ref, out_ref):
    bins = mid_ref.shape[1]
    pad = jnp.zeros((LANES - 3 * REACH, LANES), f32)
    columns = []
    for x in range(2):
        columns.append(jnp.concatenate([left_ref[x], mid_ref[x, : 2 * REACH], pad], axis=0))
    for x in range(2):
        columns.append(jnp.concatenate([mid_ref[x, bins - 2 * REACH :], right_ref[x], pad], axis=0))
    win_high, win_low = split_bf16(jnp.concatenate(columns, axis=1))
    per = 8
    best = [jnp.zeros((REACH, LANES), f32)] * 2
    for step in range(high_ref.shape[0] // (per * REACH)):
        at = slice(step * per * REACH, (step + 1) * per * REACH)
        got = products(high_ref[at, :], low_ref[at, :], win_high, win_low)
        for i in range(per):
            mine = got[i * REACH : (i + 1) * REACH]
            for side in range(2):
                lanes = slice(side * 2 * LANES, (side + 1) * 2 * LANES)
                best[side] = jnp.maximum(best[side], power(mine[:, lanes]))
    out_ref[...] = jnp.concatenate([best[0], inner_ref[...], best[1]], axis=0).T


def per_device(samples, channel_delay, merge_slope, tap_offset, tap_weight):
    freq_count = lax.axis_size("freq")
    band_count = lax.axis_size("band")
    band_pos = lax.axis_index("band")
    freq_pos = lax.axis_index("freq")
    chan_dev, samp_dev = samples.shape
    length = samp_dev * freq_count
    bins_dev = length // 2 // freq_count
    delays_sub = channel_delay.shape[1]
    block = 2 * delays_sub
    vmem = pl.BlockSpec(memory_space=pltpu.VMEM)

    first_bin = freq_pos * bins_dev
    tabs = delay_turns(channel_delay, first_bin, length)
    spread = spreading()
    bins_index = first_bin + lax.iota(jnp.int32, bins_dev)
    sections = band_count.bit_length()
    shifts = []
    for s in range(sections):
        size = 1 << s
        slope = pick_entry(merge_slope, band_pos // size * (2 * size) + size - 1)
        out_index = band_pos % size * block + lax.iota(jnp.int32, block)
        shifts.append(out_index * slope // 16 % length)
    turns = jnp.stack(
        turning(jnp.stack(shifts)[:, None, :] * bins_index[None, :, None], length), axis=1
    )
    matches = tap_offset[:, :, None] + REACH == lax.iota(jnp.int32, bins_dev)[None, None, :]
    profile = jnp.sum(jnp.where(matches, tap_weight[:, :, None], 0.0), axis=1)
    templates = profile.shape[0]
    inner_bins = bins_dev - 2 * REACH
    band_shape = jax.ShapeDtypeStruct((templates * inner_bins, bins_dev), bf16)
    edge_shape = jax.ShapeDtypeStruct((templates * REACH, LANES), bf16)
    bands = pl.pallas_call(
        toeplitz_kernel,
        out_shape=(band_shape, band_shape, edge_shape, edge_shape),
        in_specs=[vmem],
        out_specs=(vmem,) * 4,
        compiler_params=pltpu.CompilerParams(vmem_limit_bytes=40 * 2**20),
        name="toeplitz",
    )(profile)

    blocks = samples.reshape(freq_count, chan_dev // freq_count, samp_dev)
    blocks = lax.all_to_all(blocks, "freq", split_axis=0, concat_axis=0, tiled=True)
    blocks, tabs, spread, bands = lax.optimization_barrier((blocks, tabs, spread, bands))
    spec = transform(blocks, length)
    spec = lax.all_to_all(spec, "freq", split_axis=0, concat_axis=0, tiled=True)
    spec, turns = lax.optimization_barrier((spec, turns))

    current = pl.pallas_call(
        sub_kernel,
        out_shape=jax.ShapeDtypeStruct((2, bins_dev, block), f32),
        in_specs=[vmem] * 4,
        out_specs=vmem,
        scratch_shapes=[
            pltpu.VMEM((4, chan_dev, 2 * LANES), bf16),
            pltpu.VMEM((2, chan_dev // 2, LANES), f32),
            pltpu.VMEM((GROUP // 2, chan_dev, 2 * LANES), f32),
        ],
        compiler_params=pltpu.CompilerParams(vmem_limit_bytes=40 * 2**20),
        name="subband",
    )(spec, tabs, spread, turns[0])

    for s in range(1, sections):
        half = 1 << (s - 1)
        partner = lax.ppermute(current, "band", [(i, i ^ half) for i in range(band_count)])
        upper_side = band_pos % (2 * half) >= half
        lower = jnp.where(upper_side, partner, current)
        upper = jnp.where(upper_side, current, partner)
        up_re, up_im = rotate(upper[0], upper[1], turns[s, 0], turns[s, 1])
        current = jnp.stack([lower[0] + up_re, lower[1] + up_im])

    ends = freq_count - 1
    from_left = lax.ppermute(
        current[:, bins_dev - REACH :], "freq", [(i, i + 1) for i in range(ends)]
    )
    from_right = lax.ppermute(current[:, :REACH], "freq", [(i + 1, i) for i in range(ends)])
    inner = pl.pallas_call(
        inner_kernel,
        out_shape=jax.ShapeDtypeStruct((inner_bins, block), f32),
        in_specs=[vmem] * 3,
        out_specs=vmem,
        cost_estimate=pl.CostEstimate(
            flops=6 * templates * inner_bins * bins_dev * 2 * block,
            bytes_accessed=4 * templates * inner_bins * bins_dev,
            transcendentals=0,
        ),
        compiler_params=pltpu.CompilerParams(vmem_limit_bytes=40 * 2**20),
        name="inner_bins",
    )(current, bands[0], bands[1])
    return pl.pallas_call(
        edge_kernel,
        out_shape=jax.ShapeDtypeStruct((block, bins_dev), f32),
        in_specs=[vmem] * 6,
        out_specs=vmem,
        compiler_params=pltpu.CompilerParams(vmem_limit_bytes=40 * 2**20),
        name="edge_bins",
    )(from_left, current, from_right, inner, bands[2], bands[3])


def solution(mesh):
    placed = (P("band", "freq"), P("band", None), P(), P(), P())
    return jax.shard_map(
        per_device, mesh=mesh, in_specs=placed, out_specs=P("band", "freq"), check_vma=False
    )
```

```python
import functools
import math

import jax
import jax.numpy as jnp
from jax import lax
from jax.experimental import pallas as pl
from jax.experimental.pallas import tpu as pltpu
from jax.sharding import PartitionSpec as P

REACH = 32
LANES = 128
GROUP = 8
SUB_VMEM = 20 * 2**20
FILTER_VMEM = 20 * 2**20

two_pi = 2.0 * math.pi
top_precision = lax.Precision.HIGHEST
f32 = jnp.float32
bf16 = jnp.bfloat16


def turning(count, modulus):
    angle = (count % modulus).astype(f32) * (two_pi / modulus)
    return (jnp.cos(angle), jnp.sin(angle))


def rotate(real, imag, cosine, sine_part):
    return (real * cosine + imag * sine_part, imag * cosine - real * sine_part)


def pick_entry(table, index):
    return jnp.sum(jnp.where(lax.iota(jnp.int32, table.shape[0]) == index, table, 0))


def split_bf16(value):
    high = value.astype(bf16)
    return high, (value - high.astype(f32)).astype(bf16)


def transform(blocks, length):
    sources, rows, samp = blocks.shape
    inner = length // LANES
    grid = blocks.transpose(1, 0, 2).reshape(rows, inner, LANES)
    index = lax.iota(jnp.int32, LANES)
    cos_first, sin_first = turning(index[:, None] * index[None, :], inner)
    part_re = jnp.einsum("cab,ak->ckb", grid, cos_first, precision=top_precision)
    part_im = -jnp.einsum("cab,ak->ckb", grid, sin_first, precision=top_precision)
    cos_twist, sin_twist = turning(index[:, None] * index[None, :], length)
    part_re, part_im = rotate(part_re, part_im, cos_twist, sin_twist)
    column = lax.iota(jnp.int32, LANES)
    kept = column // 4 * 2 + column % 2
    imag_col = (column // 2 % 2 == 1)[None, :]
    cos_second, sin_second = turning(index[:, None] * kept[None, :], LANES)
    scale = 1.0 / math.sqrt(length) / 16.0 / 4.0
    from_re = jnp.where(imag_col, -sin_second, cos_second) * scale
    from_im = jnp.where(imag_col, cos_second, sin_second) * scale
    both = jnp.concatenate([part_re, part_im], axis=2)
    out = jnp.einsum(
        "ckb,bm->mck", both, jnp.concatenate([from_re, from_im], axis=0), precision=top_precision
    )
    return out.reshape(LANES // 4, 4, rows, LANES)


def delay_turns(channel_delay, first_bin, length):
    per_sub = channel_delay.shape[0] // 2
    both = jnp.concatenate([channel_delay[:per_sub], channel_delay[per_sub:]], axis=1)
    halves = [2 * first_bin + LANES * q + GROUP - 1 for q in range(4)]
    halves += [2 * GROUP] + [2 * b + 1 for b in range(GROUP // 2)]
    count = both[None] * jnp.stack([jnp.int32(h) for h in halves])[:, None, None]
    return jnp.stack(turning(count, 2 * length), axis=1)


def spreading():
    shape = (LANES // 2 // GROUP, GROUP // 2, 2 * LANES, 2 * LANES)
    i = [lax.broadcasted_iota(jnp.int32, shape, d) for d in range(4)]
    half = LANES // 2
    source = i[0] * GROUP + i[1] * 2 + i[3] // LANES + i[3] % LANES // half * half
    return (i[2] % LANES == source).astype(bf16)


def sub_kernel(quarters, spec_ref, tab_ref, spread_ref, tw_ref, out_ref, parts, centre, wide):
    half = LANES // 2
    per_sub = centre.shape[2]
    sources = spec_ref.shape[0] // 2
    rows = spec_ref.shape[2]
    left = lax.broadcasted_iota(jnp.int32, (rows, LANES), 1) < half

    def arrange(g, carry):
        at = pl.ds(pl.multiple_of(rows * g, rows), rows)
        for x in range(2):
            to = pl.ds(pl.multiple_of(per_sub * x + rows * g, rows), rows)
            for slot, q in enumerate(quarters):
                first = spec_ref[g, 2 * x + q // 2]
                second = spec_ref[sources + g, 2 * x + q // 2]
                if q % 2 == 0:
                    pair = jnp.where(left, first, pltpu.roll(second, half, 1))
                else:
                    pair = jnp.where(left, pltpu.roll(first, half, 1), second)
                high, low = split_bf16(pair)
                parts[slot, to, 0:LANES] = high
                parts[slot, to, LANES:] = low
                centre[slot, x, at, :] = tab_ref[q, x, at, :]
        return carry

    lax.fori_loop(0, sources, arrange, 0, unroll=2)
    steps = spread_ref.shape[0]

    def bins(step, carry):
        slot = step // steps
        for n in range(GROUP // 2):
            for r in range(2):
                at = slice(r * per_sub, (r + 1) * per_sub)
                wide[n, at, :] = jnp.dot(
                    parts[slot, at, :],
                    spread_ref[step % steps, n],
                    preferred_element_type=f32,
                )

        def channels(g, sums):
            re = list(sums[:GROUP])
            im = list(sums[GROUP:])
            at = pl.ds(pl.multiple_of(8 * g, 8), 8)
            at_im = pl.ds(pl.multiple_of(per_sub + 8 * g, 8), 8)
            mid_cos = centre[slot, 0, at, :]
            mid_sin = centre[slot, 1, at, :]
            for b in range(GROUP // 2):
                off_cos = tab_ref[5 + b, 0, at, :]
                off_sin = tab_ref[5 + b, 1, at, :]
                cc, ss = mid_cos * off_cos, mid_sin * off_sin
                sc, cs = mid_sin * off_cos, mid_cos * off_sin
                for j, cosine, sine in (
                    (GROUP // 2 + b, cc - ss, sc + cs),
                    (GROUP // 2 - 1 - b, cc + ss, sc - cs),
                ):
                    lanes = slice(j % 2 * LANES, j % 2 * LANES + LANES)
                    real = wide[j // 2, at, lanes]
                    imag = wide[j // 2, at_im, lanes]
                    re[j] = re[j] + (real * cosine + imag * sine)
                    im[j] = im[j] + (imag * cosine - real * sine)
            step_cos = tab_ref[4, 0, at, :]
            step_sin = tab_ref[4, 1, at, :]
            centre[slot, 0, at, :] = mid_cos * step_cos - mid_sin * step_sin
            centre[slot, 1, at, :] = mid_sin * step_cos + mid_cos * step_sin
            return tuple(re) + tuple(im)

        zero = jnp.zeros((8, LANES), f32)
        sums = lax.fori_loop(0, per_sub // 8, channels, (zero,) * (2 * GROUP), unroll=per_sub // 8)
        at = pl.ds(pl.multiple_of(step * GROUP, GROUP), GROUP)
        re, im = (
            jnp.concatenate(
                [jnp.sum(v, axis=0, keepdims=True) for v in sums[x * GROUP : (x + 1) * GROUP]],
                axis=0,
            )
            for x in range(2)
        )
        lower = lax.broadcasted_iota(jnp.int32, re.shape, 1) < half
        re_turn = pltpu.roll(re, half, 1)
        im_turn = pltpu.roll(im, half, 1)
        up_re, up_im = rotate(
            jnp.where(lower, re_turn, re),
            jnp.where(lower, im_turn, im),
            tw_ref[0, at, :],
            tw_ref[1, at, :],
        )
        out_ref[0, at, :] = jnp.where(lower, re, re_turn) + up_re
        out_ref[1, at, :] = jnp.where(lower, im, im_turn) + up_im
        return carry

    lax.fori_loop(0, out_ref.shape[1] // GROUP, bins, 0)


def toeplitz_kernel(profile_ref, high_ref, low_ref, edge_high_ref, edge_low_ref):
    rows = high_ref.shape[0] // profile_ref.shape[0]

    def body(a, carry):
        row = profile_ref[pl.ds(a, 1), :]
        wide = jnp.broadcast_to(row, (rows, row.shape[1]))
        high, low = split_bf16(pltpu.roll(wide, 0, 1, stride=1, stride_axis=0))
        at = pl.ds(pl.multiple_of(a * rows, rows), rows)
        high_ref[at, :] = high
        low_ref[at, :] = low
        at = pl.ds(pl.multiple_of(a * REACH, REACH), REACH)
        edge_high_ref[at, :] = high[:REACH, :LANES]
        edge_low_ref[at, :] = low[:REACH, :LANES]
        return carry

    lax.fori_loop(0, profile_ref.shape[0], body, 0)


def products(high, low, win_high, win_low):
    return (
        jnp.dot(high, win_high, preferred_element_type=f32)
        + jnp.dot(high, win_low, preferred_element_type=f32)
        + jnp.dot(low, win_high, preferred_element_type=f32)
    )


def power(value):
    re, im = value[:, :LANES], value[:, LANES:]
    return re * re + im * im


def edge_kernel(left_ref, outer_ref, right_ref, high_ref, low_ref, out_ref):
    near = 2 * REACH
    pad = jnp.zeros((LANES - 3 * REACH, LANES), f32)
    columns = [
        jnp.concatenate([left_ref[x], outer_ref[x, :near], pad], axis=0) for x in range(2)
    ] + [jnp.concatenate([outer_ref[x, near:], right_ref[x], pad], axis=0) for x in range(2)]
    win_high, win_low = split_bf16(jnp.concatenate(columns, axis=1))
    per = 8
    best = [jnp.zeros((REACH, LANES), f32)] * 2
    for step in range(high_ref.shape[0] // (per * REACH)):
        at = slice(step * per * REACH, (step + 1) * per * REACH)
        got = products(high_ref[at, :], low_ref[at, :], win_high, win_low)
        for i in range(per):
            mine = got[i * REACH : (i + 1) * REACH]
            for side in range(2):
                lanes = slice(side * 2 * LANES, (side + 1) * 2 * LANES)
                best[side] = jnp.maximum(best[side], power(mine[:, lanes]))
    out_ref[0] = best[0]
    out_ref[1] = best[1]


def inner_kernel(outer_ref, mid_ref, edge_ref, high_ref, low_ref, out_ref):
    near = 2 * REACH
    rows = out_ref.shape[1] - near
    per = 2
    columns = [
        jnp.concatenate([outer_ref[x, :near], mid_ref[x], outer_ref[x, near:]], axis=0)
        for x in range(2)
    ]
    win_high, win_low = split_bf16(jnp.concatenate(columns, axis=1))

    def body(step, best):
        at = pl.ds(pl.multiple_of(step * per * rows, rows), per * rows)
        got = products(high_ref[at, :], low_ref[at, :], win_high, win_low)
        for i in range(per):
            best = jnp.maximum(best, power(got[i * rows : (i + 1) * rows]))
        return best

    steps = high_ref.shape[0] // (per * rows)
    best = lax.fori_loop(0, steps, body, jnp.zeros((rows, LANES), f32), unroll=4)
    out_ref[...] = jnp.concatenate([edge_ref[0], best, edge_ref[1]], axis=0).T


def per_device(samples, channel_delay, merge_slope, tap_offset, tap_weight):
    freq_count = lax.axis_size("freq")
    band_count = lax.axis_size("band")
    band_pos = lax.axis_index("band")
    freq_pos = lax.axis_index("freq")
    chan_dev, samp_dev = samples.shape
    length = samp_dev * freq_count
    bins_dev = length // 2 // freq_count
    delays_sub = channel_delay.shape[1]
    block = 2 * delays_sub
    vmem = pl.BlockSpec(memory_space=pltpu.VMEM)

    first_bin = freq_pos * bins_dev
    tabs = delay_turns(channel_delay, first_bin, length)
    spread = spreading()
    sections = band_count.bit_length()
    shifts = []
    for s in range(sections):
        size = 1 << s
        slope = pick_entry(merge_slope, band_pos // size * (2 * size) + size - 1)
        out_index = band_pos % size * block + lax.iota(jnp.int32, block)
        shifts.append(out_index * slope // 16 % length)
    shifts = jnp.stack(shifts)
    chunks = ((0, 3), (1, 2))
    quarter = bins_dev // 4
    within = lax.iota(jnp.int32, quarter)
    turns = []
    for pair in chunks:
        bins_index = jnp.concatenate([first_bin + q * quarter + within for q in pair])
        count = shifts[:, None, :] * bins_index[None, :, None]
        turns.append(
            (
                jnp.stack(turning(count[0], length)),
                jnp.stack(turning(count[1:], length), axis=1),
            )
        )
    matches = tap_offset[:, :, None] + REACH == lax.iota(jnp.int32, bins_dev)[None, None, :]
    profile = jnp.sum(jnp.where(matches, tap_weight[:, :, None], 0.0), axis=1)
    templates = profile.shape[0]
    inner_bins = bins_dev - 2 * REACH
    band_shape = jax.ShapeDtypeStruct((templates * inner_bins, bins_dev), bf16)
    edge_shape = jax.ShapeDtypeStruct((templates * REACH, LANES), bf16)
    bands = pl.pallas_call(
        toeplitz_kernel,
        out_shape=(band_shape, band_shape, edge_shape, edge_shape),
        in_specs=[vmem],
        out_specs=(vmem,) * 4,
        compiler_params=pltpu.CompilerParams(vmem_limit_bytes=FILTER_VMEM),
        name="toeplitz",
    )(profile)

    blocks = samples.reshape(freq_count, chan_dev // freq_count, samp_dev)
    blocks = lax.all_to_all(blocks, "freq", split_axis=0, concat_axis=0, tiled=True)
    spec = transform(blocks, length)
    spec = lax.all_to_all(spec, "freq", split_axis=0, concat_axis=0, tiled=True)
    spec, turns, tabs, spread, bands = lax.optimization_barrier(
        (spec, turns, tabs, spread, bands)
    )

    current = []
    for pair, turn in zip(chunks, turns):
        current.append(
            pl.pallas_call(
                functools.partial(sub_kernel, pair),
                out_shape=jax.ShapeDtypeStruct((2, bins_dev // 2, block), f32),
                in_specs=[vmem] * 4,
                out_specs=vmem,
                scratch_shapes=[
                    pltpu.VMEM((2, chan_dev, 2 * LANES), bf16),
                    pltpu.VMEM((2, 2, chan_dev // 2, LANES), f32),
                    pltpu.VMEM((GROUP // 2, chan_dev, 2 * LANES), f32),
                ],
                cost_estimate=pl.CostEstimate(
                    flops=10**10, bytes_accessed=2**23, transcendentals=0
                ),
                compiler_params=pltpu.CompilerParams(vmem_limit_bytes=SUB_VMEM),
                name="subband",
            )(spec, tabs, spread, turn[0])
        )

    for s in range(1, sections):
        half = 1 << (s - 1)
        for i in range(len(chunks)):
            mine = current[i]
            partner = lax.ppermute(mine, "band", [(j, j ^ half) for j in range(band_count)])
            upper_side = band_pos % (2 * half) >= half
            lower = jnp.where(upper_side, partner, mine)
            upper = jnp.where(upper_side, mine, partner)
            turn = turns[i][1][s - 1]
            up_re, up_im = rotate(upper[0], upper[1], turn[0], turn[1])
            current[i] = jnp.stack([lower[0] + up_re, lower[1] + up_im])

    outer, middle = current
    ends = freq_count - 1
    from_left = lax.ppermute(
        outer[:, bins_dev // 2 - REACH :], "freq", [(i, i + 1) for i in range(ends)]
    )
    from_right = lax.ppermute(outer[:, :REACH], "freq", [(i + 1, i) for i in range(ends)])
    edges = pl.pallas_call(
        edge_kernel,
        out_shape=jax.ShapeDtypeStruct((2, REACH, block), f32),
        in_specs=[vmem] * 5,
        out_specs=vmem,
        compiler_params=pltpu.CompilerParams(vmem_limit_bytes=FILTER_VMEM),
        name="edge_bins",
    )(from_left, outer, from_right, bands[2], bands[3])
    return pl.pallas_call(
        inner_kernel,
        out_shape=jax.ShapeDtypeStruct((block, bins_dev), f32),
        in_specs=[vmem] * 5,
        out_specs=vmem,
        compiler_params=pltpu.CompilerParams(vmem_limit_bytes=FILTER_VMEM),
        name="inner_bins",
    )(outer, middle, edges, bands[0], bands[1])


def solution(mesh):
    placed = (P("band", "freq"), P("band", None), P(), P(), P())
    return jax.shard_map(
        per_device, mesh=mesh, in_specs=placed, out_specs=P("band", "freq"), check_vma=False
    )
```

```python
import functools
import math

import jax
import jax.numpy as jnp
from jax import lax
from jax.experimental import pallas as pl
from jax.experimental.pallas import tpu as pltpu
from jax.sharding import PartitionSpec as P

REACH = 32
LANES = 128
GROUP = 8
SUB_VMEM = 12 * 2**20
FILTER_VMEM = 8 * 2**20

two_pi = 2.0 * math.pi
top_precision = lax.Precision.HIGHEST
f32 = jnp.float32
bf16 = jnp.bfloat16


def turning(count, modulus):
    angle = (count % modulus).astype(f32) * (two_pi / modulus)
    return (jnp.cos(angle), jnp.sin(angle))


def turning_pair(count, modulus, axis):
    quarter_back = jnp.array([0, modulus // 4 * 3], jnp.int32)
    offset = quarter_back.reshape([2 if i == axis else 1 for i in range(count.ndim + 1)])
    return turning(jnp.expand_dims(count, axis) + offset, modulus)[0]


def rotate(real, imag, cosine, sine_part):
    return (real * cosine + imag * sine_part, imag * cosine - real * sine_part)


def pick_entry(table, index):
    return jnp.sum(jnp.where(lax.iota(jnp.int32, table.shape[0]) == index, table, 0))


def split_bf16(value):
    high = value.astype(bf16)
    return high, (value - high.astype(f32)).astype(bf16)


def transform(blocks, length):
    sources, rows, samp = blocks.shape
    inner = length // LANES
    grid = blocks.transpose(1, 0, 2).reshape(rows, inner, LANES)
    index = lax.iota(jnp.int32, LANES)
    cos_first, sin_first = turning(index[:, None] * index[None, :], inner)
    part_re = jnp.einsum("cab,ak->ckb", grid, cos_first, precision=top_precision)
    part_im = -jnp.einsum("cab,ak->ckb", grid, sin_first, precision=top_precision)
    cos_twist, sin_twist = turning(index[:, None] * index[None, :], length)
    part_re, part_im = rotate(part_re, part_im, cos_twist, sin_twist)
    column = lax.iota(jnp.int32, LANES)
    kept = column // 4 * 2 + column % 2
    imag_col = (column // 2 % 2 == 1)[None, :]
    cos_second, sin_second = turning(index[:, None] * kept[None, :], LANES)
    scale = 1.0 / math.sqrt(length) / 16.0 / 4.0
    from_re = jnp.where(imag_col, -sin_second, cos_second) * scale
    from_im = jnp.where(imag_col, cos_second, sin_second) * scale
    both = jnp.concatenate([part_re, part_im], axis=2)
    out = jnp.einsum(
        "ckb,bm->mck", both, jnp.concatenate([from_re, from_im], axis=0), precision=top_precision
    )
    return out.reshape(LANES // 4, 4, rows, LANES)


def delay_turns(channel_delay, first_bin, length):
    per_sub = channel_delay.shape[0] // 2
    both = jnp.concatenate([channel_delay[:per_sub], channel_delay[per_sub:]], axis=1)
    halves = [2 * first_bin + LANES * q + GROUP - 1 for q in range(4)]
    halves += [2 * GROUP] + [2 * b + 1 for b in range(GROUP // 2)]
    count = both[None] * jnp.stack([jnp.int32(h) for h in halves])[:, None, None]
    return turning_pair(count, 2 * length, 1)


def spreading():
    shape = (LANES // 2 // GROUP, GROUP // 2, LANES, 2 * LANES)
    i = [lax.broadcasted_iota(jnp.int32, shape, d) for d in range(4)]
    half = LANES // 2
    source = i[0] * GROUP + i[1] * 2 + i[3] // LANES + i[3] % LANES // half * half
    return (i[2] == source).astype(bf16)


def sub_kernel(quarters, spec_ref, tab_ref, spread_ref, tw_ref, out_ref, parts, centre, wide):
    half = LANES // 2
    per_sub = centre.shape[2]
    sources = spec_ref.shape[0] // 2
    rows = spec_ref.shape[2]
    left = lax.broadcasted_iota(jnp.int32, (rows, LANES), 1) < half

    def arrange(g, carry):
        at = pl.ds(pl.multiple_of(rows * g, rows), rows)
        for x in range(2):
            to = pl.ds(pl.multiple_of(per_sub * x + rows * g, rows), rows)
            for slot, q in enumerate(quarters):
                first = spec_ref[g, 2 * x + q // 2]
                second = spec_ref[sources + g, 2 * x + q // 2]
                if q % 2 == 0:
                    pair = jnp.where(left, first, pltpu.roll(second, half, 1))
                else:
                    pair = jnp.where(left, pltpu.roll(first, half, 1), second)
                high, low = split_bf16(pair)
                parts[slot, to, 0:LANES] = high
                parts[slot, to, LANES:] = low
                centre[slot, x, at, :] = tab_ref[q, x, at, :]
        return carry

    lax.fori_loop(0, sources, arrange, 0, unroll=2)
    steps = spread_ref.shape[0]

    def bins(step, carry):
        slot = step // steps
        for n in range(GROUP // 2):
            one_hot = spread_ref[step % steps, n]
            one_hot = jnp.concatenate([one_hot, one_hot], axis=0)
            for r in range(2):
                at = slice(r * per_sub, (r + 1) * per_sub)
                wide[n, at, :] = jnp.dot(
                    parts[slot, at, :],
                    one_hot,
                    preferred_element_type=f32,
                )

        def channels(g, sums):
            re = list(sums[:GROUP])
            im = list(sums[GROUP:])
            at = pl.ds(pl.multiple_of(8 * g, 8), 8)
            at_im = pl.ds(pl.multiple_of(per_sub + 8 * g, 8), 8)
            mid_cos = centre[slot, 0, at, :]
            mid_sin = centre[slot, 1, at, :]
            for b in range(GROUP // 2):
                off_cos = tab_ref[5 + b, 0, at, :]
                off_sin = tab_ref[5 + b, 1, at, :]
                cc, ss = mid_cos * off_cos, mid_sin * off_sin
                sc, cs = mid_sin * off_cos, mid_cos * off_sin
                for j, cosine, sine in (
                    (GROUP // 2 + b, cc - ss, sc + cs),
                    (GROUP // 2 - 1 - b, cc + ss, sc - cs),
                ):
                    lanes = slice(j % 2 * LANES, j % 2 * LANES + LANES)
                    real = wide[j // 2, at, lanes]
                    imag = wide[j // 2, at_im, lanes]
                    re[j] = re[j] + (real * cosine + imag * sine)
                    im[j] = im[j] + (imag * cosine - real * sine)
            step_cos = tab_ref[4, 0, at, :]
            step_sin = tab_ref[4, 1, at, :]
            centre[slot, 0, at, :] = mid_cos * step_cos - mid_sin * step_sin
            centre[slot, 1, at, :] = mid_sin * step_cos + mid_cos * step_sin
            return tuple(re) + tuple(im)

        zero = jnp.zeros((8, LANES), f32)
        sums = lax.fori_loop(0, per_sub // 8, channels, (zero,) * (2 * GROUP), unroll=per_sub // 8)
        at = pl.ds(pl.multiple_of(step * GROUP, GROUP), GROUP)
        re, im = (
            jnp.concatenate(
                [jnp.sum(v, axis=0, keepdims=True) for v in sums[x * GROUP : (x + 1) * GROUP]],
                axis=0,
            )
            for x in range(2)
        )
        lower = lax.broadcasted_iota(jnp.int32, re.shape, 1) < half
        re_turn = pltpu.roll(re, half, 1)
        im_turn = pltpu.roll(im, half, 1)
        up_re, up_im = rotate(
            jnp.where(lower, re_turn, re),
            jnp.where(lower, im_turn, im),
            tw_ref[0, at, :],
            tw_ref[1, at, :],
        )
        out_ref[0, at, :] = jnp.where(lower, re, re_turn) + up_re
        out_ref[1, at, :] = jnp.where(lower, im, im_turn) + up_im
        return carry

    lax.fori_loop(0, out_ref.shape[1] // GROUP, bins, 0)


def toeplitz_kernel(profile_ref, band_ref):
    rows = 2 * REACH

    def body(a, carry):
        row = profile_ref[pl.ds(a, 1), :]
        wide = jnp.broadcast_to(row, (rows, row.shape[1]))
        high, low = split_bf16(pltpu.roll(wide, 0, 1, stride=1, stride_axis=0))
        at = pl.ds(pl.multiple_of(a * rows, rows), rows)
        band_ref[at, :LANES] = high
        band_ref[at, LANES:] = low
        return carry

    lax.fori_loop(0, profile_ref.shape[0], body, 0, unroll=4)


def windows(value):
    high, low = split_bf16(value)
    return jnp.concatenate([high, high], axis=0), jnp.concatenate([low, low], axis=0)


def products(band, high, low):
    return jnp.dot(band, high, preferred_element_type=f32) + jnp.dot(
        band, low, preferred_element_type=f32
    )


def power(value):
    re, im = value[:, :LANES], value[:, LANES:]
    return re * re + im * im


def edge_kernel(left_ref, outer_ref, right_ref, band_ref, out_ref):
    near = 2 * REACH
    pad = jnp.zeros((LANES - 3 * REACH, LANES), f32)
    columns = [
        jnp.concatenate([left_ref[x], outer_ref[x, :near], pad], axis=0) for x in range(2)
    ] + [jnp.concatenate([outer_ref[x, near:], right_ref[x], pad], axis=0) for x in range(2)]
    high, low = windows(jnp.concatenate(columns, axis=1))
    per = 8
    best = [jnp.zeros((REACH, LANES), f32)] * 2
    for step in range(band_ref.shape[0] // (per * near)):
        first = step * per * near
        band = jnp.concatenate(
            [band_ref[first + i * near : first + i * near + REACH, :] for i in range(per)], axis=0
        )
        got = products(band, high, low)
        for i in range(per):
            mine = got[i * REACH : (i + 1) * REACH]
            for side in range(2):
                lanes = slice(side * 2 * LANES, (side + 1) * 2 * LANES)
                best[side] = jnp.maximum(best[side], power(mine[:, lanes]))
    out_ref[0] = best[0]
    out_ref[1] = best[1]


def inner_kernel(outer_ref, mid_ref, edge_ref, band_ref, out_ref):
    near = 2 * REACH
    blocks = out_ref.shape[1] // near - 1
    columns = [
        jnp.concatenate([outer_ref[x, :near], mid_ref[x], outer_ref[x, near:]], axis=0)
        for x in range(2)
    ]
    whole = jnp.concatenate(columns, axis=1)
    per = 4
    best = []
    for i in range(blocks):
        high, low = windows(whole[i * near : i * near + LANES])
        mine = jnp.zeros((near, LANES), f32)
        for step in range(band_ref.shape[0] // (per * near)):
            at = slice(step * per * near, (step + 1) * per * near)
            got = products(band_ref[at, :], high, low)
            for j in range(per):
                mine = jnp.maximum(mine, power(got[j * near : (j + 1) * near]))
        best.append(mine)
    out_ref[...] = jnp.concatenate([edge_ref[0]] + best + [edge_ref[1]], axis=0).T


def per_device(samples, channel_delay, merge_slope, tap_offset, tap_weight):
    freq_count = lax.axis_size("freq")
    band_count = lax.axis_size("band")
    band_pos = lax.axis_index("band")
    freq_pos = lax.axis_index("freq")
    chan_dev, samp_dev = samples.shape
    length = samp_dev * freq_count
    bins_dev = length // 2 // freq_count
    delays_sub = channel_delay.shape[1]
    block = 2 * delays_sub
    vmem = pl.BlockSpec(memory_space=pltpu.VMEM)

    first_bin = freq_pos * bins_dev
    tabs = delay_turns(channel_delay, first_bin, length)
    spread = spreading()
    sections = band_count.bit_length()
    shifts = []
    for s in range(sections):
        size = 1 << s
        slope = pick_entry(merge_slope, band_pos // size * (2 * size) + size - 1)
        out_index = band_pos % size * block + lax.iota(jnp.int32, block)
        shifts.append(out_index * slope // 16 % length)
    shifts = jnp.stack(shifts)
    chunks = ((0, 3), (1, 2))
    quarter = bins_dev // 4
    within = lax.iota(jnp.int32, quarter)
    turns = []
    for pair in chunks:
        bins_index = jnp.concatenate([first_bin + q * quarter + within for q in pair])
        count = shifts[:, None, :] * bins_index[None, :, None]
        turns.append(
            (
                turning_pair(count[0], length, 0),
                turning_pair(count[1:], length, 1),
            )
        )
    matches = tap_offset[:, :, None] + REACH == lax.iota(jnp.int32, LANES)[None, None, :]
    profile = jnp.sum(jnp.where(matches, tap_weight[:, :, None], 0.0), axis=1)
    templates = profile.shape[0]
    band = pl.pallas_call(
        toeplitz_kernel,
        out_shape=jax.ShapeDtypeStruct((templates * 2 * REACH, 2 * LANES), bf16),
        in_specs=[vmem],
        out_specs=vmem,
        compiler_params=pltpu.CompilerParams(vmem_limit_bytes=FILTER_VMEM),
        name="toeplitz",
    )(profile)

    blocks = samples.reshape(freq_count, chan_dev // freq_count, samp_dev)
    blocks = lax.all_to_all(blocks, "freq", split_axis=0, concat_axis=0, tiled=True)
    spec = transform(blocks, length)
    spec = lax.all_to_all(spec, "freq", split_axis=0, concat_axis=0, tiled=True)
    spec, turns, tabs, spread, band = lax.optimization_barrier(
        (spec, turns, tabs, spread, band)
    )

    current = []
    for pair, turn in zip(chunks, turns):
        current.append(
            pl.pallas_call(
                functools.partial(sub_kernel, pair),
                out_shape=jax.ShapeDtypeStruct((2, bins_dev // 2, block), f32),
                in_specs=[vmem] * 4,
                out_specs=vmem,
                scratch_shapes=[
                    pltpu.VMEM((2, chan_dev, 2 * LANES), bf16),
                    pltpu.VMEM((2, 2, chan_dev // 2, LANES), f32),
                    pltpu.VMEM((GROUP // 2, chan_dev, 2 * LANES), f32),
                ],
                cost_estimate=pl.CostEstimate(
                    flops=10**10, bytes_accessed=2**23, transcendentals=0
                ),
                compiler_params=pltpu.CompilerParams(vmem_limit_bytes=SUB_VMEM),
                name="subband",
            )(spec, tabs, spread, turn[0])
        )

    for s in range(1, sections):
        half = 1 << (s - 1)
        for i in range(len(chunks)):
            mine = current[i]
            partner = lax.ppermute(mine, "band", [(j, j ^ half) for j in range(band_count)])
            upper_side = band_pos % (2 * half) >= half
            lower = jnp.where(upper_side, partner, mine)
            upper = jnp.where(upper_side, mine, partner)
            turn = turns[i][1][s - 1]
            up_re, up_im = rotate(upper[0], upper[1], turn[0], turn[1])
            current[i] = jnp.stack([lower[0] + up_re, lower[1] + up_im])

    outer, middle = current
    ends = freq_count - 1
    from_left = lax.ppermute(
        outer[:, bins_dev // 2 - REACH :], "freq", [(i, i + 1) for i in range(ends)]
    )
    from_right = lax.ppermute(outer[:, :REACH], "freq", [(i + 1, i) for i in range(ends)])
    edges = pl.pallas_call(
        edge_kernel,
        out_shape=jax.ShapeDtypeStruct((2, REACH, block), f32),
        in_specs=[vmem] * 4,
        out_specs=vmem,
        compiler_params=pltpu.CompilerParams(vmem_limit_bytes=FILTER_VMEM),
        name="edge_bins",
    )(from_left, outer, from_right, band)
    return pl.pallas_call(
        inner_kernel,
        out_shape=jax.ShapeDtypeStruct((block, bins_dev), f32),
        in_specs=[vmem] * 4,
        out_specs=vmem,
        compiler_params=pltpu.CompilerParams(vmem_limit_bytes=FILTER_VMEM),
        name="inner_bins",
    )(outer, middle, edges, band)


def solution(mesh):
    placed = (P("band", "freq"), P("band", None), P(), P(), P())
    return jax.shard_map(
        per_device, mesh=mesh, in_specs=placed, out_specs=P("band", "freq"), check_vma=False
    )
```

```python
import functools
import math

import jax
import jax.numpy as jnp
from jax import lax
from jax.experimental import pallas as pl
from jax.experimental.pallas import tpu as pltpu
from jax.sharding import PartitionSpec as P

REACH = 32
LANES = 128
GROUP = 8
SUB_VMEM = 12 * 2**20
FILTER_VMEM = 8 * 2**20

two_pi = 2.0 * math.pi
f32 = jnp.float32
bf16 = jnp.bfloat16


def turning(count, modulus):
    angle = (count % modulus).astype(f32) * (two_pi / modulus)
    return (jnp.cos(angle), jnp.sin(angle))


def turning_pair(count, modulus, axis):
    quarter_back = jnp.array([0, modulus // 4 * 3], jnp.int32)
    offset = quarter_back.reshape([2 if i == axis else 1 for i in range(count.ndim + 1)])
    return turning(jnp.expand_dims(count, axis) + offset, modulus)[0]


def rotate(real, imag, cosine, sine_part):
    return (real * cosine + imag * sine_part, imag * cosine - real * sine_part)


def pick_entry(table, index):
    return jnp.sum(jnp.where(lax.iota(jnp.int32, table.shape[0]) == index, table, 0))


def split_bf16(value):
    high = value.astype(bf16)
    return high, (value - high.astype(f32)).astype(bf16)


def transform_tables(length):
    inner = length // LANES
    index = lax.iota(jnp.int32, LANES)
    sources = LANES // 4
    block_no = index % sources * 4 + index // sources
    cos_first, sin_first = turning(index[:, None] * block_no[None, :], inner)
    first = jnp.concatenate([cos_first, -sin_first], axis=0)
    twist = turning_pair(index[:, None] * index[None, :], length, 0)
    kept = index // 4 * 2 + index % 2
    imag_row = (index // 2 % 2 == 1)[:, None]
    cos_second, sin_second = turning(kept[:, None] * index[None, :], LANES)
    scale = 1.0 / math.sqrt(length) / 16.0 / 4.0
    from_re = jnp.where(imag_row, -sin_second, cos_second) * scale
    from_im = jnp.where(imag_row, cos_second, sin_second) * scale
    return first, twist, jnp.concatenate([from_re, from_im], axis=1)


def transform_kernel(blocks_ref, first_ref, twist_ref, second_ref, out_ref, tall):
    channels = out_ref.shape[0] // LANES
    held = blocks_ref.shape[0]
    for r in range(blocks_ref.shape[1] // LANES):
        tall[r * held : (r + 1) * held, :] = blocks_ref[:, r * LANES : (r + 1) * LANES]
    first = jnp.concatenate(split_bf16(first_ref[...]), axis=1)
    second_high, second_low = split_bf16(second_ref[...])
    second = jnp.concatenate([second_high, second_low], axis=0)
    across = (((1,), (1,)), ((), ()))
    for pair in range(channels // 2):
        mine = (2 * pair, 2 * pair + 1)
        columns = [tall[pl.ds(c, LANES, stride=channels), :] for c in mine]
        part = products(first, *windows(jnp.concatenate(columns, axis=1)))
        rows = []
        for j in range(2):
            lanes = slice(j * LANES, (j + 1) * LANES)
            turned = rotate(part[:LANES, lanes], part[LANES:, lanes], twist_ref[0], twist_ref[1])
            rows.append(jnp.concatenate(turned, axis=1))
        high, low = split_bf16(jnp.concatenate(rows, axis=0))
        got = lax.dot_general(second, high, across, preferred_element_type=f32)
        got = (
            got[:LANES]
            + got[LANES:]
            + lax.dot_general(second_high, low, across, preferred_element_type=f32)
        )
        for j, c in enumerate(mine):
            out_ref[pl.ds(c, LANES, stride=channels), :] = got[:, j * LANES : (j + 1) * LANES]


def delay_turns(channel_delay, first_bin, length):
    per_sub = channel_delay.shape[0] // 2
    both = jnp.concatenate([channel_delay[:per_sub], channel_delay[per_sub:]], axis=1)
    halves = [2 * first_bin + LANES * q + GROUP - 1 for q in range(4)]
    halves += [2 * GROUP] + [2 * b + 1 for b in range(GROUP // 2)]
    count = both[None] * jnp.stack([jnp.int32(h) for h in halves])[:, None, None]
    return turning_pair(count, 2 * length, 1)


def spreading():
    shape = (LANES // 2 // GROUP, GROUP // 2, LANES, 2 * LANES)
    i = [lax.broadcasted_iota(jnp.int32, shape, d) for d in range(4)]
    half = LANES // 2
    source = i[0] * GROUP + i[1] * 2 + i[3] // LANES + i[3] % LANES // half * half
    return (i[2] == source).astype(bf16)


def sub_kernel(quarters, spec_ref, tab_ref, spread_ref, tw_ref, out_ref, parts, centre, wide):
    half = LANES // 2
    per_sub = centre.shape[2]
    sources = spec_ref.shape[0] // 2
    rows = spec_ref.shape[2]
    left = lax.broadcasted_iota(jnp.int32, (rows, LANES), 1) < half

    def arrange(g, carry):
        at = pl.ds(pl.multiple_of(rows * g, rows), rows)
        for x in range(2):
            to = pl.ds(pl.multiple_of(per_sub * x + rows * g, rows), rows)
            for slot, q in enumerate(quarters):
                first = spec_ref[g, 2 * x + q // 2]
                second = spec_ref[sources + g, 2 * x + q // 2]
                if q % 2 == 0:
                    pair = jnp.where(left, first, pltpu.roll(second, half, 1))
                else:
                    pair = jnp.where(left, pltpu.roll(first, half, 1), second)
                high, low = split_bf16(pair)
                parts[slot, to, 0:LANES] = high
                parts[slot, to, LANES:] = low
                centre[slot, x, at, :] = tab_ref[q, x, at, :]
        return carry

    lax.fori_loop(0, sources, arrange, 0, unroll=2)
    steps = spread_ref.shape[0]

    def bins(step, carry):
        slot = step // steps
        for n in range(GROUP // 2):
            one_hot = spread_ref[step % steps, n]
            one_hot = jnp.concatenate([one_hot, one_hot], axis=0)
            for r in range(2):
                at = slice(r * per_sub, (r + 1) * per_sub)
                wide[n, at, :] = jnp.dot(
                    parts[slot, at, :],
                    one_hot,
                    preferred_element_type=f32,
                )

        def channels(g, sums):
            re = list(sums[:GROUP])
            im = list(sums[GROUP:])
            at = pl.ds(pl.multiple_of(8 * g, 8), 8)
            at_im = pl.ds(pl.multiple_of(per_sub + 8 * g, 8), 8)
            mid_cos = centre[slot, 0, at, :]
            mid_sin = centre[slot, 1, at, :]
            for b in range(GROUP // 2):
                off_cos = tab_ref[5 + b, 0, at, :]
                off_sin = tab_ref[5 + b, 1, at, :]
                cc, ss = mid_cos * off_cos, mid_sin * off_sin
                sc, cs = mid_sin * off_cos, mid_cos * off_sin
                for j, cosine, sine in (
                    (GROUP // 2 + b, cc - ss, sc + cs),
                    (GROUP // 2 - 1 - b, cc + ss, sc - cs),
                ):
                    lanes = slice(j % 2 * LANES, j % 2 * LANES + LANES)
                    real = wide[j // 2, at, lanes]
                    imag = wide[j // 2, at_im, lanes]
                    re[j] = re[j] + (real * cosine + imag * sine)
                    im[j] = im[j] + (imag * cosine - real * sine)
            step_cos = tab_ref[4, 0, at, :]
            step_sin = tab_ref[4, 1, at, :]
            centre[slot, 0, at, :] = mid_cos * step_cos - mid_sin * step_sin
            centre[slot, 1, at, :] = mid_sin * step_cos + mid_cos * step_sin
            return tuple(re) + tuple(im)

        zero = jnp.zeros((8, LANES), f32)
        sums = lax.fori_loop(0, per_sub // 8, channels, (zero,) * (2 * GROUP), unroll=per_sub // 8)
        at = pl.ds(pl.multiple_of(step * GROUP, GROUP), GROUP)
        re, im = (
            jnp.concatenate(
                [jnp.sum(v, axis=0, keepdims=True) for v in sums[x * GROUP : (x + 1) * GROUP]],
                axis=0,
            )
            for x in range(2)
        )
        lower = lax.broadcasted_iota(jnp.int32, re.shape, 1) < half
        re_turn = pltpu.roll(re, half, 1)
        im_turn = pltpu.roll(im, half, 1)
        up_re, up_im = rotate(
            jnp.where(lower, re_turn, re),
            jnp.where(lower, im_turn, im),
            tw_ref[0, at, :],
            tw_ref[1, at, :],
        )
        out_ref[0, at, :] = jnp.where(lower, re, re_turn) + up_re
        out_ref[1, at, :] = jnp.where(lower, im, im_turn) + up_im
        return carry

    lax.fori_loop(0, out_ref.shape[1] // GROUP, bins, 0)


def toeplitz_kernel(profile_ref, band_ref):
    rows = 2 * REACH

    def body(a, carry):
        row = profile_ref[pl.ds(a, 1), :]
        wide = jnp.broadcast_to(row, (rows, row.shape[1]))
        high, low = split_bf16(pltpu.roll(wide, 0, 1, stride=1, stride_axis=0))
        at = pl.ds(pl.multiple_of(a * rows, rows), rows)
        band_ref[at, :LANES] = high
        band_ref[at, LANES:] = low
        return carry

    lax.fori_loop(0, profile_ref.shape[0], body, 0, unroll=4)


def windows(value):
    high, low = split_bf16(value)
    return jnp.concatenate([high, high], axis=0), jnp.concatenate([low, low], axis=0)


def products(band, high, low):
    return jnp.dot(band, high, preferred_element_type=f32) + jnp.dot(
        band, low, preferred_element_type=f32
    )


def power(value):
    re, im = value[:, :LANES], value[:, LANES:]
    return re * re + im * im


def filter_kernel(outer_ref, rest_ref, band_ref, out_ref):
    near = 2 * REACH
    mid = rest_ref.shape[1] - near
    columns = [
        jnp.concatenate(
            [
                rest_ref[x, mid : mid + REACH],
                outer_ref[x, :near],
                rest_ref[x, :mid],
                outer_ref[x, near:],
                rest_ref[x, mid + REACH :],
            ],
            axis=0,
        )
        for x in range(2)
    ]
    whole = jnp.concatenate(columns, axis=1)
    per = 4
    best = []
    for i in range(out_ref.shape[1] // near):
        high, low = windows(whole[i * near : i * near + LANES])
        mine = jnp.zeros((near, LANES), f32)
        for step in range(band_ref.shape[0] // (per * near)):
            at = slice(step * per * near, (step + 1) * per * near)
            got = products(band_ref[at, :], high, low)
            for j in range(per):
                mine = jnp.maximum(mine, power(got[j * near : (j + 1) * near]))
        best.append(mine)
    out_ref[...] = jnp.concatenate(best, axis=0).T


def per_device(samples, channel_delay, merge_slope, tap_offset, tap_weight):
    freq_count = lax.axis_size("freq")
    band_count = lax.axis_size("band")
    band_pos = lax.axis_index("band")
    freq_pos = lax.axis_index("freq")
    chan_dev, samp_dev = samples.shape
    length = samp_dev * freq_count
    bins_dev = length // 2 // freq_count
    delays_sub = channel_delay.shape[1]
    block = 2 * delays_sub
    vmem = pl.BlockSpec(memory_space=pltpu.VMEM)

    first_bin = freq_pos * bins_dev
    tabs = delay_turns(channel_delay, first_bin, length)
    spread = spreading()
    sections = band_count.bit_length()
    shifts = []
    for s in range(sections):
        size = 1 << s
        slope = pick_entry(merge_slope, band_pos // size * (2 * size) + size - 1)
        out_index = band_pos % size * block + lax.iota(jnp.int32, block)
        shifts.append(out_index * slope // 16 % length)
    shifts = jnp.stack(shifts)
    chunks = ((0, 3), (1, 2))
    quarter = bins_dev // 4
    within = lax.iota(jnp.int32, quarter)
    turns = []
    for pair in chunks:
        bins_index = jnp.concatenate([first_bin + q * quarter + within for q in pair])
        if pair == chunks[1]:
            reach = lax.iota(jnp.int32, REACH)
            bins_index = jnp.concatenate(
                [bins_index, first_bin - REACH + reach, first_bin + bins_dev + reach]
            )
        count = shifts[:, None, :] * bins_index[None, :, None]
        turns.append(
            (
                turning_pair(count[0, : 2 * quarter], length, 0),
                turning_pair(count[1:], length, 1),
            )
        )
    matches = tap_offset[:, :, None] + REACH == lax.iota(jnp.int32, LANES)[None, None, :]
    profile = jnp.sum(jnp.where(matches, tap_weight[:, :, None], 0.0), axis=1)
    templates = profile.shape[0]
    band = pl.pallas_call(
        toeplitz_kernel,
        out_shape=jax.ShapeDtypeStruct((templates * 2 * REACH, 2 * LANES), bf16),
        in_specs=[vmem],
        out_specs=vmem,
        compiler_params=pltpu.CompilerParams(vmem_limit_bytes=FILTER_VMEM),
        name="toeplitz",
    )(profile)

    tables = transform_tables(length)
    blocks = samples.reshape(freq_count, chan_dev // freq_count, samp_dev)
    blocks = lax.all_to_all(blocks, "freq", split_axis=0, concat_axis=0, tiled=True)
    spec = pl.pallas_call(
        transform_kernel,
        out_shape=jax.ShapeDtypeStruct((chan_dev // freq_count * LANES, LANES), f32),
        in_specs=[vmem] * 4,
        out_specs=vmem,
        scratch_shapes=[pltpu.VMEM((chan_dev // freq_count * LANES, LANES), f32)],
        compiler_params=pltpu.CompilerParams(vmem_limit_bytes=FILTER_VMEM),
        name="transform",
    )(blocks.reshape(chan_dev, samp_dev), *tables)
    spec = spec.reshape(freq_count, chan_dev * 4 // freq_count, LANES)
    spec = lax.all_to_all(spec, "freq", split_axis=0, concat_axis=0, tiled=True)
    spec = spec.reshape(freq_count, 4, chan_dev // freq_count, LANES)
    spec, turns, tabs, spread, band = lax.optimization_barrier(
        (spec, turns, tabs, spread, band)
    )

    current = []
    for pair, turn in zip(chunks, turns):
        current.append(
            pl.pallas_call(
                functools.partial(sub_kernel, pair),
                out_shape=jax.ShapeDtypeStruct((2, bins_dev // 2, block), f32),
                in_specs=[vmem] * 4,
                out_specs=vmem,
                scratch_shapes=[
                    pltpu.VMEM((2, chan_dev, 2 * LANES), bf16),
                    pltpu.VMEM((2, 2, chan_dev // 2, LANES), f32),
                    pltpu.VMEM((GROUP // 2, chan_dev, 2 * LANES), f32),
                ],
                cost_estimate=pl.CostEstimate(
                    flops=10**10, bytes_accessed=2**23, transcendentals=0
                ),
                compiler_params=pltpu.CompilerParams(vmem_limit_bytes=SUB_VMEM),
                name="subband",
            )(spec, tabs, spread, turn[0])
        )

    ends = freq_count - 1
    from_left = lax.ppermute(
        current[0][:, bins_dev // 2 - REACH :], "freq", [(i, i + 1) for i in range(ends)]
    )
    from_right = lax.ppermute(current[0][:, :REACH], "freq", [(i + 1, i) for i in range(ends)])
    current[1] = jnp.concatenate([current[1], from_left, from_right], axis=1)
    for s in range(1, sections):
        half = 1 << (s - 1)
        for i in range(len(chunks)):
            mine = current[i]
            partner = lax.ppermute(mine, "band", [(j, j ^ half) for j in range(band_count)])
            upper_side = band_pos % (2 * half) >= half
            lower = jnp.where(upper_side, partner, mine)
            upper = jnp.where(upper_side, mine, partner)
            turn = turns[i][1][s - 1]
            up_re, up_im = rotate(upper[0], upper[1], turn[0], turn[1])
            current[i] = jnp.stack([lower[0] + up_re, lower[1] + up_im])

    return pl.pallas_call(
        filter_kernel,
        out_shape=jax.ShapeDtypeStruct((block, bins_dev), f32),
        in_specs=[vmem] * 3,
        out_specs=vmem,
        compiler_params=pltpu.CompilerParams(vmem_limit_bytes=FILTER_VMEM),
        name="templates",
    )(current[0], current[1], band)


def solution(mesh):
    placed = (P("band", "freq"), P("band", None), P(), P(), P())
    return jax.shard_map(
        per_device, mesh=mesh, in_specs=placed, out_specs=P("band", "freq"), check_vma=False
    )
```

```python
import functools
import math

import jax
import jax.numpy as jnp
from jax import lax
from jax.experimental import pallas as pl
from jax.experimental.pallas import tpu as pltpu
from jax.sharding import PartitionSpec as P

REACH = 32
LANES = 128
GROUP = 8
SUB_VMEM = 12 * 2**20
FILTER_VMEM = 8 * 2**20

two_pi = 2.0 * math.pi
f32 = jnp.float32
bf16 = jnp.bfloat16


def turning(count, modulus):
    angle = (count % modulus).astype(f32) * (two_pi / modulus)
    return (jnp.cos(angle), jnp.sin(angle))


def turning_pair(count, modulus, axis):
    quarter_back = jnp.array([0, modulus // 4 * 3], jnp.int32)
    offset = quarter_back.reshape([2 if i == axis else 1 for i in range(count.ndim + 1)])
    return turning(jnp.expand_dims(count, axis) + offset, modulus)[0]


def rotate(real, imag, cosine, sine_part):
    return (real * cosine + imag * sine_part, imag * cosine - real * sine_part)


def pick_entry(table, index):
    return jnp.sum(jnp.where(lax.iota(jnp.int32, table.shape[0]) == index, table, 0))


def split_bf16(value):
    high = value.astype(bf16)
    return high, (value - high.astype(f32)).astype(bf16)


def transform_tables(length):
    inner = length // LANES
    index = lax.iota(jnp.int32, LANES)
    sources = LANES // 4
    block_no = index % sources * 4 + index // sources
    cos_first, sin_first = turning(index[:, None] * block_no[None, :], inner)
    first = jnp.concatenate([cos_first, -sin_first], axis=0)
    twist = turning_pair(index[:, None] * index[None, :], length, 0)
    kept = index // 4 * 2 + index % 2
    imag_row = (index // 2 % 2 == 1)[:, None]
    cos_second, sin_second = turning(kept[:, None] * index[None, :], LANES)
    scale = 1.0 / math.sqrt(length) / 16.0 / 4.0
    from_re = jnp.where(imag_row, -sin_second, cos_second) * scale
    from_im = jnp.where(imag_row, cos_second, sin_second) * scale
    return first, twist, jnp.concatenate([from_re, from_im], axis=1)


def transform_kernel(blocks_ref, first_ref, twist_ref, second_ref, out_ref, tall):
    channels = out_ref.shape[0] // LANES
    held = blocks_ref.shape[0]
    for r in range(blocks_ref.shape[1] // LANES):
        tall[r * held : (r + 1) * held, :] = blocks_ref[:, r * LANES : (r + 1) * LANES]
    first = jnp.concatenate(split_bf16(first_ref[...]), axis=1)
    second_high, second_low = split_bf16(second_ref[...])
    second = jnp.concatenate([second_high, second_low], axis=0)
    across = (((1,), (1,)), ((), ()))
    for pair in range(channels // 2):
        mine = (2 * pair, 2 * pair + 1)
        columns = [tall[pl.ds(c, LANES, stride=channels), :] for c in mine]
        part = products(first, *windows(jnp.concatenate(columns, axis=1)))
        rows = []
        for j in range(2):
            lanes = slice(j * LANES, (j + 1) * LANES)
            turned = rotate(part[:LANES, lanes], part[LANES:, lanes], twist_ref[0], twist_ref[1])
            rows.append(jnp.concatenate(turned, axis=1))
        high, low = split_bf16(jnp.concatenate(rows, axis=0))
        got = lax.dot_general(second, high, across, preferred_element_type=f32)
        got = (
            got[:LANES]
            + got[LANES:]
            + lax.dot_general(second_high, low, across, preferred_element_type=f32)
        )
        for j, c in enumerate(mine):
            out_ref[pl.ds(c, LANES, stride=channels), :] = got[:, j * LANES : (j + 1) * LANES]


def delay_turns(channel_delay, first_bin, length):
    per_sub = channel_delay.shape[0] // 2
    both = jnp.concatenate([channel_delay[:per_sub], channel_delay[per_sub:]], axis=1)
    halves = [2 * first_bin + GROUP - 1, 2 * GROUP, 1]
    count = both[None] * jnp.stack([jnp.int32(h) for h in halves])[:, None, None]
    return turning_pair(count, 2 * length, 1)


def add_angles(a, b):
    return (a[0] * b[0] - a[1] * b[1], a[1] * b[0] + a[0] * b[1])


def sub_kernel(
    quarters, spec_ref, tab_ref, tw_ref, out_ref, parts, centre, wide, offset, spread
):
    half = LANES // 2
    per_sub = centre.shape[2]
    sources = spec_ref.shape[0] // 2
    rows = spec_ref.shape[2]
    left = lax.broadcasted_iota(jnp.int32, (rows, LANES), 1) < half

    def arrange(g, carry):
        at = pl.ds(pl.multiple_of(rows * g, rows), rows)
        for x in range(2):
            to = pl.ds(pl.multiple_of(per_sub * x + rows * g, rows), rows)
            for slot, q in enumerate(quarters):
                first = spec_ref[g, 2 * x + q // 2]
                second = spec_ref[sources + g, 2 * x + q // 2]
                if q % 2 == 0:
                    pair = jnp.where(left, first, pltpu.roll(second, half, 1))
                else:
                    pair = jnp.where(left, pltpu.roll(first, half, 1), second)
                high, low = split_bf16(pair)
                parts[slot, to, 0:LANES] = high
                parts[slot, to, LANES:] = low
        first, step, unit = ((tab_ref[i, 0, at, :], tab_ref[i, 1, at, :]) for i in range(3))
        bin_turn = add_angles(unit, unit)
        for b in range(GROUP // 2):
            offset[b, 0, at, :], offset[b, 1, at, :] = unit
            unit = add_angles(unit, bin_turn)
        for _ in range(3):
            step = add_angles(step, step)
        for q in range(4):
            if q in quarters:
                slot = quarters.index(q)
                centre[slot, 0, at, :], centre[slot, 1, at, :] = first
            first = add_angles(first, step)
        return carry

    lax.fori_loop(0, sources, arrange, 0, unroll=2)
    steps = half // GROUP
    source = lax.broadcasted_iota(jnp.int32, (LANES, 2 * LANES), 0)
    target = lax.broadcasted_iota(jnp.int32, (LANES, 2 * LANES), 1)
    apart = source - target // LANES - target % LANES // half * half

    def one_hots(n, carry):
        spread[n] = jnp.where(apart == 2 * n, 1.0, 0.0).astype(bf16)
        return carry

    lax.fori_loop(0, spread.shape[0], one_hots, 0)

    def bins(step, carry):
        slot = step // steps
        for n in range(GROUP // 2):
            one_hot = spread[step % steps * (GROUP // 2) + n]
            one_hot = jnp.concatenate([one_hot, one_hot], axis=0)
            for r in range(2):
                at = slice(r * per_sub, (r + 1) * per_sub)
                wide[n, at, :] = jnp.dot(
                    parts[slot, at, :],
                    one_hot,
                    preferred_element_type=f32,
                )

        def channels(g, sums):
            re = list(sums[:GROUP])
            im = list(sums[GROUP:])
            at = pl.ds(pl.multiple_of(8 * g, 8), 8)
            at_im = pl.ds(pl.multiple_of(per_sub + 8 * g, 8), 8)
            mid_cos = centre[slot, 0, at, :]
            mid_sin = centre[slot, 1, at, :]
            for b in range(GROUP // 2):
                off_cos = offset[b, 0, at, :]
                off_sin = offset[b, 1, at, :]
                cc, ss = mid_cos * off_cos, mid_sin * off_sin
                sc, cs = mid_sin * off_cos, mid_cos * off_sin
                for j, cosine, sine in (
                    (GROUP // 2 + b, cc - ss, sc + cs),
                    (GROUP // 2 - 1 - b, cc + ss, sc - cs),
                ):
                    lanes = slice(j % 2 * LANES, j % 2 * LANES + LANES)
                    real = wide[j // 2, at, lanes]
                    imag = wide[j // 2, at_im, lanes]
                    re[j] = re[j] + (real * cosine + imag * sine)
                    im[j] = im[j] + (imag * cosine - real * sine)
            step_cos = tab_ref[1, 0, at, :]
            step_sin = tab_ref[1, 1, at, :]
            centre[slot, 0, at, :] = mid_cos * step_cos - mid_sin * step_sin
            centre[slot, 1, at, :] = mid_sin * step_cos + mid_cos * step_sin
            return tuple(re) + tuple(im)

        zero = jnp.zeros((8, LANES), f32)
        sums = lax.fori_loop(0, per_sub // 8, channels, (zero,) * (2 * GROUP), unroll=per_sub // 8)
        at = pl.ds(pl.multiple_of(step * GROUP, GROUP), GROUP)
        re, im = (
            jnp.concatenate(
                [jnp.sum(v, axis=0, keepdims=True) for v in sums[x * GROUP : (x + 1) * GROUP]],
                axis=0,
            )
            for x in range(2)
        )
        lower = lax.broadcasted_iota(jnp.int32, re.shape, 1) < half
        re_turn = pltpu.roll(re, half, 1)
        im_turn = pltpu.roll(im, half, 1)
        up_re, up_im = rotate(
            jnp.where(lower, re_turn, re),
            jnp.where(lower, im_turn, im),
            tw_ref[0, at, :],
            tw_ref[1, at, :],
        )
        out_ref[0, at, :] = jnp.where(lower, re, re_turn) + up_re
        out_ref[1, at, :] = jnp.where(lower, im, im_turn) + up_im
        return carry

    lax.fori_loop(0, out_ref.shape[1] // GROUP, bins, 0)


def toeplitz_kernel(profile_ref, band_ref):
    rows = 2 * REACH

    def body(a, carry):
        row = profile_ref[pl.ds(a, 1), :]
        wide = jnp.broadcast_to(row, (rows, row.shape[1]))
        high, low = split_bf16(pltpu.roll(wide, 0, 1, stride=1, stride_axis=0))
        at = pl.ds(pl.multiple_of(a * rows, rows), rows)
        band_ref[at, :LANES] = high
        band_ref[at, LANES:] = low
        return carry

    lax.fori_loop(0, profile_ref.shape[0], body, 0, unroll=4)


def windows(value):
    high, low = split_bf16(value)
    return jnp.concatenate([high, high], axis=0), jnp.concatenate([low, low], axis=0)


def products(band, high, low):
    return jnp.dot(band, high, preferred_element_type=f32) + jnp.dot(
        band, low, preferred_element_type=f32
    )


def power(value):
    re, im = value[:, :LANES], value[:, LANES:]
    return re * re + im * im


def edge_kernel(left_ref, outer_ref, right_ref, band_ref, out_ref):
    near = 2 * REACH
    pad = jnp.zeros((LANES - 3 * REACH, LANES), f32)
    columns = [
        jnp.concatenate([left_ref[x], outer_ref[x, :near], pad], axis=0) for x in range(2)
    ] + [jnp.concatenate([outer_ref[x, near:], right_ref[x], pad], axis=0) for x in range(2)]
    high, low = windows(jnp.concatenate(columns, axis=1))
    per = 8
    best = [jnp.zeros((REACH, LANES), f32)] * 2
    for step in range(band_ref.shape[0] // (per * near)):
        first = step * per * near
        band = jnp.concatenate(
            [band_ref[first + i * near : first + i * near + REACH, :] for i in range(per)], axis=0
        )
        got = products(band, high, low)
        for i in range(per):
            mine = got[i * REACH : (i + 1) * REACH]
            for side in range(2):
                lanes = slice(side * 2 * LANES, (side + 1) * 2 * LANES)
                best[side] = jnp.maximum(best[side], power(mine[:, lanes]))
    out_ref[0] = best[0]
    out_ref[1] = best[1]


def inner_kernel(outer_ref, mid_ref, edge_ref, band_ref, out_ref):
    near = 2 * REACH
    blocks = out_ref.shape[1] // near - 1
    columns = [
        jnp.concatenate([outer_ref[x, :near], mid_ref[x], outer_ref[x, near:]], axis=0)
        for x in range(2)
    ]
    whole = jnp.concatenate(columns, axis=1)
    per = 4
    best = []
    for i in range(blocks):
        high, low = windows(whole[i * near : i * near + LANES])
        mine = jnp.zeros((near, LANES), f32)
        for step in range(band_ref.shape[0] // (per * near)):
            at = slice(step * per * near, (step + 1) * per * near)
            got = products(band_ref[at, :], high, low)
            for j in range(per):
                mine = jnp.maximum(mine, power(got[j * near : (j + 1) * near]))
        best.append(mine)
    out_ref[...] = jnp.concatenate([edge_ref[0]] + best + [edge_ref[1]], axis=0).T


def per_device(samples, channel_delay, merge_slope, tap_offset, tap_weight):
    freq_count = lax.axis_size("freq")
    band_count = lax.axis_size("band")
    band_pos = lax.axis_index("band")
    freq_pos = lax.axis_index("freq")
    chan_dev, samp_dev = samples.shape
    length = samp_dev * freq_count
    bins_dev = length // 2 // freq_count
    delays_sub = channel_delay.shape[1]
    block = 2 * delays_sub
    vmem = pl.BlockSpec(memory_space=pltpu.VMEM)

    first_bin = freq_pos * bins_dev
    tabs = delay_turns(channel_delay, first_bin, length)
    sections = band_count.bit_length()
    shifts = []
    for s in range(sections):
        size = 1 << s
        slope = pick_entry(merge_slope, band_pos // size * (2 * size) + size - 1)
        out_index = band_pos % size * block + lax.iota(jnp.int32, block)
        shifts.append(out_index * slope // 16 % length)
    shifts = jnp.stack(shifts)
    chunks = ((0, 3), (1, 2))
    quarter = bins_dev // 4
    within = lax.iota(jnp.int32, quarter)
    turns = []
    for pair in chunks:
        bins_index = jnp.concatenate([first_bin + q * quarter + within for q in pair])
        count = shifts[:, None, :] * bins_index[None, :, None]
        turns.append(
            (
                turning_pair(count[0], length, 0),
                turning_pair(count[1:], length, 1),
            )
        )
    matches = tap_offset[:, :, None] + REACH == lax.iota(jnp.int32, LANES)[None, None, :]
    profile = jnp.sum(jnp.where(matches, tap_weight[:, :, None], 0.0), axis=1)
    templates = profile.shape[0]
    band = pl.pallas_call(
        toeplitz_kernel,
        out_shape=jax.ShapeDtypeStruct((templates * 2 * REACH, 2 * LANES), bf16),
        in_specs=[vmem],
        out_specs=vmem,
        compiler_params=pltpu.CompilerParams(vmem_limit_bytes=FILTER_VMEM),
        name="toeplitz",
    )(profile)

    tables = transform_tables(length)
    blocks = samples.reshape(freq_count, chan_dev // freq_count, samp_dev)
    blocks = lax.all_to_all(blocks, "freq", split_axis=0, concat_axis=0, tiled=True)
    spec = pl.pallas_call(
        transform_kernel,
        out_shape=jax.ShapeDtypeStruct((chan_dev // freq_count * LANES, LANES), f32),
        in_specs=[vmem] * 4,
        out_specs=vmem,
        scratch_shapes=[pltpu.VMEM((chan_dev // freq_count * LANES, LANES), f32)],
        compiler_params=pltpu.CompilerParams(vmem_limit_bytes=FILTER_VMEM),
        name="transform",
    )(blocks.reshape(chan_dev, samp_dev), *tables)
    spec = spec.reshape(freq_count, chan_dev * 4 // freq_count, LANES)
    spec = lax.all_to_all(spec, "freq", split_axis=0, concat_axis=0, tiled=True)
    spec = spec.reshape(freq_count, 4, chan_dev // freq_count, LANES)
    spec, turns, tabs, band = lax.optimization_barrier((spec, turns, tabs, band))

    current = []
    for pair, turn in zip(chunks, turns):
        current.append(
            pl.pallas_call(
                functools.partial(sub_kernel, pair),
                out_shape=jax.ShapeDtypeStruct((2, bins_dev // 2, block), f32),
                in_specs=[vmem] * 3,
                out_specs=vmem,
                scratch_shapes=[
                    pltpu.VMEM((2, chan_dev, 2 * LANES), bf16),
                    pltpu.VMEM((2, 2, chan_dev // 2, LANES), f32),
                    pltpu.VMEM((GROUP // 2, chan_dev, 2 * LANES), f32),
                    pltpu.VMEM((GROUP // 2, 2, chan_dev // 2, LANES), f32),
                    pltpu.VMEM((LANES // 4, LANES, 2 * LANES), bf16),
                ],
                cost_estimate=pl.CostEstimate(
                    flops=10**10, bytes_accessed=2**23, transcendentals=0
                ),
                compiler_params=pltpu.CompilerParams(vmem_limit_bytes=SUB_VMEM),
                name="subband",
            )(spec, tabs, turn[0])
        )

    for s in range(1, sections):
        half = 1 << (s - 1)
        for i in range(len(chunks)):
            mine = current[i]
            partner = lax.ppermute(mine, "band", [(j, j ^ half) for j in range(band_count)])
            upper_side = band_pos % (2 * half) >= half
            lower = jnp.where(upper_side, partner, mine)
            upper = jnp.where(upper_side, mine, partner)
            turn = turns[i][1][s - 1]
            up_re, up_im = rotate(upper[0], upper[1], turn[0], turn[1])
            current[i] = jnp.stack([lower[0] + up_re, lower[1] + up_im])

    outer, middle = current
    ends = freq_count - 1
    from_left = lax.ppermute(
        outer[:, bins_dev // 2 - REACH :], "freq", [(i, i + 1) for i in range(ends)]
    )
    from_right = lax.ppermute(outer[:, :REACH], "freq", [(i + 1, i) for i in range(ends)])
    edges = pl.pallas_call(
        edge_kernel,
        out_shape=jax.ShapeDtypeStruct((2, REACH, block), f32),
        in_specs=[vmem] * 4,
        out_specs=vmem,
        compiler_params=pltpu.CompilerParams(vmem_limit_bytes=FILTER_VMEM),
        name="edge_bins",
    )(from_left, outer, from_right, band)
    return pl.pallas_call(
        inner_kernel,
        out_shape=jax.ShapeDtypeStruct((block, bins_dev), f32),
        in_specs=[vmem] * 4,
        out_specs=vmem,
        compiler_params=pltpu.CompilerParams(vmem_limit_bytes=FILTER_VMEM),
        name="inner_bins",
    )(outer, middle, edges, band)


def solution(mesh):
    placed = (P("band", "freq"), P("band", None), P(), P(), P())
    return jax.shard_map(
        per_device, mesh=mesh, in_specs=placed, out_specs=P("band", "freq"), check_vma=False
    )
```

```python
import functools
import math

import jax
import jax.numpy as jnp
from jax import lax
from jax.experimental import pallas as pl
from jax.experimental.pallas import tpu as pltpu
from jax.sharding import PartitionSpec as P

REACH = 32
LANES = 128
GROUP = 8
SUB_VMEM = 14 * 2**20
FILTER_VMEM = 8 * 2**20

two_pi = 2.0 * math.pi
f32 = jnp.float32
bf16 = jnp.bfloat16


def turning(count, modulus):
    angle = (count % modulus).astype(f32) * (two_pi / modulus)
    return (jnp.cos(angle), jnp.sin(angle))


def turning_pair(count, modulus, axis):
    quarter_back = jnp.array([0, modulus // 4 * 3], jnp.int32)
    offset = quarter_back.reshape([2 if i == axis else 1 for i in range(count.ndim + 1)])
    return turning(jnp.expand_dims(count, axis) + offset, modulus)[0]


def rotate(real, imag, cosine, sine_part):
    return (real * cosine + imag * sine_part, imag * cosine - real * sine_part)


def pick_entry(table, index):
    return jnp.sum(jnp.where(lax.iota(jnp.int32, table.shape[0]) == index, table, 0))


def split_bf16(value):
    high = value.astype(bf16)
    return high, (value - high.astype(f32)).astype(bf16)


def transform_tables(length):
    inner = length // LANES
    index = lax.iota(jnp.int32, LANES)
    sources = LANES // 4
    block_no = index % sources * 4 + index // sources
    cos_first, sin_first = turning(index[:, None] * block_no[None, :], inner)
    first = jnp.concatenate([cos_first, -sin_first], axis=0)
    twist = turning_pair(index[:, None] * index[None, :], length, 0)
    kept = index // 4 * 2 + index % 2
    imag_row = (index // 2 % 2 == 1)[:, None]
    cos_second, sin_second = turning(kept[:, None] * index[None, :], LANES)
    scale = 1.0 / math.sqrt(length) / 16.0 / 4.0
    from_re = jnp.where(imag_row, -sin_second, cos_second) * scale
    from_im = jnp.where(imag_row, cos_second, sin_second) * scale
    return first, twist, jnp.concatenate([from_re, from_im], axis=1)


def transform_kernel(blocks_ref, first_ref, twist_ref, second_ref, out_ref, tall):
    channels = out_ref.shape[0] // LANES
    held = blocks_ref.shape[0]
    for r in range(blocks_ref.shape[1] // LANES):
        tall[r * held : (r + 1) * held, :] = blocks_ref[:, r * LANES : (r + 1) * LANES]
    first = jnp.concatenate(split_bf16(first_ref[...]), axis=1)
    second_high, second_low = split_bf16(second_ref[...])
    second = jnp.concatenate([second_high, second_low], axis=0)
    across = (((1,), (1,)), ((), ()))
    for pair in range(channels // 2):
        mine = (2 * pair, 2 * pair + 1)
        columns = [tall[pl.ds(c, LANES, stride=channels), :] for c in mine]
        part = products(first, *windows(jnp.concatenate(columns, axis=1)))
        rows = []
        for j in range(2):
            lanes = slice(j * LANES, (j + 1) * LANES)
            turned = rotate(part[:LANES, lanes], part[LANES:, lanes], twist_ref[0], twist_ref[1])
            rows.append(jnp.concatenate(turned, axis=1))
        high, low = split_bf16(jnp.concatenate(rows, axis=0))
        got = lax.dot_general(second, high, across, preferred_element_type=f32)
        got = (
            got[:LANES]
            + got[LANES:]
            + lax.dot_general(second_high, low, across, preferred_element_type=f32)
        )
        for j, c in enumerate(mine):
            out_ref[pl.ds(c, LANES, stride=channels), :] = got[:, j * LANES : (j + 1) * LANES]


def delay_turns(channel_delay, first_bin, length):
    per_sub = channel_delay.shape[0] // 2
    both = jnp.concatenate([channel_delay[:per_sub], channel_delay[per_sub:]], axis=1)
    halves = [2 * first_bin + GROUP - 1, 2 * GROUP, 1]
    count = both[None] * jnp.stack([jnp.int32(h) for h in halves])[:, None, None]
    return turning_pair(count, 2 * length, 1)


def add_angles(a, b):
    return (a[0] * b[0] - a[1] * b[1], a[1] * b[0] + a[0] * b[1])


def sub_kernel(
    quarters, spec_ref, tab_ref, tw_ref, out_ref, parts, centre, wide, offset, spread
):
    half = LANES // 2
    per_sub = centre.shape[2]
    sources = spec_ref.shape[0] // 2
    rows = spec_ref.shape[2]
    left = lax.broadcasted_iota(jnp.int32, (rows, LANES), 1) < half

    def arrange(g, carry):
        at = pl.ds(pl.multiple_of(rows * g, rows), rows)
        for x in range(2):
            to = pl.ds(pl.multiple_of(per_sub * x + rows * g, rows), rows)
            for slot, q in enumerate(quarters):
                first = spec_ref[g, 2 * x + q // 2]
                second = spec_ref[sources + g, 2 * x + q // 2]
                if q % 2 == 0:
                    pair = jnp.where(left, first, pltpu.roll(second, half, 1))
                else:
                    pair = jnp.where(left, pltpu.roll(first, half, 1), second)
                high, low = split_bf16(pair)
                parts[slot, to, 0:LANES] = high
                parts[slot, to, LANES:] = low
        first, step, unit = ((tab_ref[i, 0, at, :], tab_ref[i, 1, at, :]) for i in range(3))
        bin_turn = add_angles(unit, unit)
        for b in range(GROUP // 2):
            offset[b, 0, at, :], offset[b, 1, at, :] = unit
            unit = add_angles(unit, bin_turn)
        for _ in range(3):
            step = add_angles(step, step)
        for q in range(4):
            if q in quarters:
                slot = quarters.index(q)
                centre[slot, 0, at, :], centre[slot, 1, at, :] = first
            first = add_angles(first, step)
        return carry

    lax.fori_loop(0, sources, arrange, 0, unroll=2)
    passes = half // (2 * GROUP)
    source = lax.broadcasted_iota(jnp.int32, (LANES, 2 * LANES), 0)
    target = lax.broadcasted_iota(jnp.int32, (LANES, 2 * LANES), 1)
    apart = source - target // LANES - target % LANES // half * half

    def one_hots(n, carry):
        spread[n] = jnp.where(apart == 2 * n, 1.0, 0.0).astype(bf16)
        return carry

    lax.fori_loop(0, spread.shape[0], one_hots, 0)

    def bins(step, carry):
        slot = step // passes
        for n in range(GROUP):
            one_hot = spread[step % passes * GROUP + n]
            one_hot = jnp.concatenate([one_hot, one_hot], axis=0)
            for r in range(2):
                at = slice(r * per_sub, (r + 1) * per_sub)
                wide[n, at, :] = jnp.dot(
                    parts[slot, at, :],
                    one_hot,
                    preferred_element_type=f32,
                )

        def channels(g, sums):
            re = list(sums[: 2 * GROUP])
            im = list(sums[2 * GROUP :])
            at = pl.ds(pl.multiple_of(8 * g, 8), 8)
            at_im = pl.ds(pl.multiple_of(per_sub + 8 * g, 8), 8)
            advance = (tab_ref[1, 0, at, :], tab_ref[1, 1, at, :])
            mids = [(centre[slot, 0, at, :], centre[slot, 1, at, :])]
            mids.append(add_angles(mids[0], advance))
            for b in range(GROUP // 2):
                off_cos = offset[b, 0, at, :]
                off_sin = offset[b, 1, at, :]
                for h, (mid_cos, mid_sin) in enumerate(mids):
                    cc, ss = mid_cos * off_cos, mid_sin * off_sin
                    sc, cs = mid_sin * off_cos, mid_cos * off_sin
                    for j, cosine, sine in (
                        (h * GROUP + GROUP // 2 + b, cc - ss, sc + cs),
                        (h * GROUP + GROUP // 2 - 1 - b, cc + ss, sc - cs),
                    ):
                        lanes = slice(j % 2 * LANES, j % 2 * LANES + LANES)
                        real = wide[j // 2, at, lanes]
                        imag = wide[j // 2, at_im, lanes]
                        re[j] = re[j] + (real * cosine + imag * sine)
                        im[j] = im[j] + (imag * cosine - real * sine)
            centre[slot, 0, at, :], centre[slot, 1, at, :] = add_angles(mids[1], advance)
            return tuple(re) + tuple(im)

        zero = jnp.zeros((8, LANES), f32)
        sums = lax.fori_loop(0, per_sub // 8, channels, (zero,) * (4 * GROUP), unroll=per_sub // 8)
        at = pl.ds(pl.multiple_of(step * 2 * GROUP, 2 * GROUP), 2 * GROUP)
        re, im = (
            jnp.concatenate(
                [
                    jnp.sum(v, axis=0, keepdims=True)
                    for v in sums[x * 2 * GROUP : (x + 1) * 2 * GROUP]
                ],
                axis=0,
            )
            for x in range(2)
        )
        lower = lax.broadcasted_iota(jnp.int32, re.shape, 1) < half
        re_turn = pltpu.roll(re, half, 1)
        im_turn = pltpu.roll(im, half, 1)
        up_re, up_im = rotate(
            jnp.where(lower, re_turn, re),
            jnp.where(lower, im_turn, im),
            tw_ref[0, at, :],
            tw_ref[1, at, :],
        )
        out_ref[0, at, :] = jnp.where(lower, re, re_turn) + up_re
        out_ref[1, at, :] = jnp.where(lower, im, im_turn) + up_im
        return carry

    lax.fori_loop(0, out_ref.shape[1] // (2 * GROUP), bins, 0)


def toeplitz_kernel(profile_ref, band_ref):
    rows = 2 * REACH

    def body(a, carry):
        row = profile_ref[pl.ds(a, 1), :]
        wide = jnp.broadcast_to(row, (rows, row.shape[1]))
        high, low = split_bf16(pltpu.roll(wide, 0, 1, stride=1, stride_axis=0))
        at = pl.ds(pl.multiple_of(a * rows, rows), rows)
        band_ref[at, :LANES] = high
        band_ref[at, LANES:] = low
        return carry

    lax.fori_loop(0, profile_ref.shape[0], body, 0, unroll=4)


def windows(value):
    high, low = split_bf16(value)
    return jnp.concatenate([high, high], axis=0), jnp.concatenate([low, low], axis=0)


def products(band, high, low):
    return jnp.dot(band, high, preferred_element_type=f32) + jnp.dot(
        band, low, preferred_element_type=f32
    )


def power(value):
    re, im = value[:, :LANES], value[:, LANES:]
    return re * re + im * im


def edge_kernel(left_ref, outer_ref, right_ref, band_ref, out_ref):
    near = 2 * REACH
    pad = jnp.zeros((LANES - 3 * REACH, LANES), f32)
    columns = [
        jnp.concatenate([left_ref[x], outer_ref[x, :near], pad], axis=0) for x in range(2)
    ] + [jnp.concatenate([outer_ref[x, near:], right_ref[x], pad], axis=0) for x in range(2)]
    high, low = windows(jnp.concatenate(columns, axis=1))
    per = 8
    best = [jnp.zeros((REACH, LANES), f32)] * 2
    for step in range(band_ref.shape[0] // (per * near)):
        first = step * per * near
        band = jnp.concatenate(
            [band_ref[first + i * near : first + i * near + REACH, :] for i in range(per)], axis=0
        )
        got = products(band, high, low)
        for i in range(per):
            mine = got[i * REACH : (i + 1) * REACH]
            for side in range(2):
                lanes = slice(side * 2 * LANES, (side + 1) * 2 * LANES)
                best[side] = jnp.maximum(best[side], power(mine[:, lanes]))
    out_ref[0] = best[0]
    out_ref[1] = best[1]


def inner_kernel(outer_ref, mid_ref, edge_ref, band_ref, out_ref):
    near = 2 * REACH
    blocks = out_ref.shape[1] // near - 1
    columns = [
        jnp.concatenate([outer_ref[x, :near], mid_ref[x], outer_ref[x, near:]], axis=0)
        for x in range(2)
    ]
    whole = jnp.concatenate(columns, axis=1)
    per = 4
    best = []
    for i in range(blocks):
        high, low = windows(whole[i * near : i * near + LANES])
        mine = jnp.zeros((near, LANES), f32)
        for step in range(band_ref.shape[0] // (per * near)):
            at = slice(step * per * near, (step + 1) * per * near)
            got = products(band_ref[at, :], high, low)
            for j in range(per):
                mine = jnp.maximum(mine, power(got[j * near : (j + 1) * near]))
        best.append(mine)
    out_ref[...] = jnp.concatenate([edge_ref[0]] + best + [edge_ref[1]], axis=0).T


def per_device(samples, channel_delay, merge_slope, tap_offset, tap_weight):
    freq_count = lax.axis_size("freq")
    band_count = lax.axis_size("band")
    band_pos = lax.axis_index("band")
    freq_pos = lax.axis_index("freq")
    chan_dev, samp_dev = samples.shape
    length = samp_dev * freq_count
    bins_dev = length // 2 // freq_count
    delays_sub = channel_delay.shape[1]
    block = 2 * delays_sub
    vmem = pl.BlockSpec(memory_space=pltpu.VMEM)

    first_bin = freq_pos * bins_dev
    tabs = delay_turns(channel_delay, first_bin, length)
    sections = band_count.bit_length()
    shifts = []
    for s in range(sections):
        size = 1 << s
        slope = pick_entry(merge_slope, band_pos // size * (2 * size) + size - 1)
        out_index = band_pos % size * block + lax.iota(jnp.int32, block)
        shifts.append(out_index * slope // 16 % length)
    shifts = jnp.stack(shifts)
    chunks = ((0, 3), (1, 2))
    quarter = bins_dev // 4
    within = lax.iota(jnp.int32, quarter)
    turns = []
    for pair in chunks:
        bins_index = jnp.concatenate([first_bin + q * quarter + within for q in pair])
        count = shifts[:, None, :] * bins_index[None, :, None]
        turns.append(
            (
                turning_pair(count[0], length, 0),
                turning_pair(count[1:], length, 1),
            )
        )
    matches = tap_offset[:, :, None] + REACH == lax.iota(jnp.int32, LANES)[None, None, :]
    profile = jnp.sum(jnp.where(matches, tap_weight[:, :, None], 0.0), axis=1)
    templates = profile.shape[0]
    band = pl.pallas_call(
        toeplitz_kernel,
        out_shape=jax.ShapeDtypeStruct((templates * 2 * REACH, 2 * LANES), bf16),
        in_specs=[vmem],
        out_specs=vmem,
        compiler_params=pltpu.CompilerParams(vmem_limit_bytes=FILTER_VMEM),
        name="toeplitz",
    )(profile)

    tables = transform_tables(length)
    blocks = samples.reshape(freq_count, chan_dev // freq_count, samp_dev)
    blocks = lax.all_to_all(blocks, "freq", split_axis=0, concat_axis=0, tiled=True)
    spec = pl.pallas_call(
        transform_kernel,
        out_shape=jax.ShapeDtypeStruct((chan_dev // freq_count * LANES, LANES), f32),
        in_specs=[vmem] * 4,
        out_specs=vmem,
        scratch_shapes=[pltpu.VMEM((chan_dev // freq_count * LANES, LANES), f32)],
        compiler_params=pltpu.CompilerParams(vmem_limit_bytes=FILTER_VMEM),
        name="transform",
    )(blocks.reshape(chan_dev, samp_dev), *tables)
    spec = spec.reshape(freq_count, chan_dev * 4 // freq_count, LANES)
    spec = lax.all_to_all(spec, "freq", split_axis=0, concat_axis=0, tiled=True)
    spec = spec.reshape(freq_count, 4, chan_dev // freq_count, LANES)
    spec, turns, tabs, band = lax.optimization_barrier((spec, turns, tabs, band))

    current = []
    for pair, turn in zip(chunks, turns):
        current.append(
            pl.pallas_call(
                functools.partial(sub_kernel, pair),
                out_shape=jax.ShapeDtypeStruct((2, bins_dev // 2, block), f32),
                in_specs=[vmem] * 3,
                out_specs=vmem,
                scratch_shapes=[
                    pltpu.VMEM((2, chan_dev, 2 * LANES), bf16),
                    pltpu.VMEM((2, 2, chan_dev // 2, LANES), f32),
                    pltpu.VMEM((GROUP, chan_dev, 2 * LANES), f32),
                    pltpu.VMEM((GROUP // 2, 2, chan_dev // 2, LANES), f32),
                    pltpu.VMEM((LANES // 4, LANES, 2 * LANES), bf16),
                ],
                cost_estimate=pl.CostEstimate(
                    flops=10**10, bytes_accessed=2**23, transcendentals=0
                ),
                compiler_params=pltpu.CompilerParams(vmem_limit_bytes=SUB_VMEM),
                name="subband",
            )(spec, tabs, turn[0])
        )

    for s in range(1, sections):
        half = 1 << (s - 1)
        for i in range(len(chunks)):
            mine = current[i]
            partner = lax.ppermute(mine, "band", [(j, j ^ half) for j in range(band_count)])
            upper_side = band_pos % (2 * half) >= half
            lower = jnp.where(upper_side, partner, mine)
            upper = jnp.where(upper_side, mine, partner)
            turn = turns[i][1][s - 1]
            up_re, up_im = rotate(upper[0], upper[1], turn[0], turn[1])
            current[i] = jnp.stack([lower[0] + up_re, lower[1] + up_im])

    outer, middle = current
    ends = freq_count - 1
    from_left = lax.ppermute(
        outer[:, bins_dev // 2 - REACH :], "freq", [(i, i + 1) for i in range(ends)]
    )
    from_right = lax.ppermute(outer[:, :REACH], "freq", [(i + 1, i) for i in range(ends)])
    edges = pl.pallas_call(
        edge_kernel,
        out_shape=jax.ShapeDtypeStruct((2, REACH, block), f32),
        in_specs=[vmem] * 4,
        out_specs=vmem,
        compiler_params=pltpu.CompilerParams(vmem_limit_bytes=FILTER_VMEM),
        name="edge_bins",
    )(from_left, outer, from_right, band)
    return pl.pallas_call(
        inner_kernel,
        out_shape=jax.ShapeDtypeStruct((block, bins_dev), f32),
        in_specs=[vmem] * 4,
        out_specs=vmem,
        compiler_params=pltpu.CompilerParams(vmem_limit_bytes=FILTER_VMEM),
        name="inner_bins",
    )(outer, middle, edges, band)


def solution(mesh):
    placed = (P("band", "freq"), P("band", None), P(), P(), P())
    return jax.shard_map(
        per_device, mesh=mesh, in_specs=placed, out_specs=P("band", "freq"), check_vma=False
    )
```

```python
import functools
import math

import jax
import jax.numpy as jnp
from jax import lax
from jax.experimental import pallas as pl
from jax.experimental.pallas import tpu as pltpu
from jax.sharding import PartitionSpec as P

REACH = 32
LANES = 128
GROUP = 8
SUB_VMEM = 14 * 2**20
FILTER_VMEM = 8 * 2**20

two_pi = 2.0 * math.pi
f32 = jnp.float32
bf16 = jnp.bfloat16


def turning(count, modulus):
    angle = (count % modulus).astype(f32) * (two_pi / modulus)
    return (jnp.cos(angle), jnp.sin(angle))


def turning_pair(count, modulus, axis):
    quarter_back = jnp.array([0, modulus // 4 * 3], jnp.int32)
    offset = quarter_back.reshape([2 if i == axis else 1 for i in range(count.ndim + 1)])
    return turning(jnp.expand_dims(count, axis) + offset, modulus)[0]


def rotate(real, imag, cosine, sine_part):
    return (real * cosine + imag * sine_part, imag * cosine - real * sine_part)


def pick_entry(table, index):
    return jnp.sum(jnp.where(lax.iota(jnp.int32, table.shape[0]) == index, table, 0))


def split_bf16(value):
    high = value.astype(bf16)
    return high, (value - high.astype(f32)).astype(bf16)


def transform_tables(length):
    inner = length // LANES
    index = lax.iota(jnp.int32, LANES)
    sources = LANES // 4
    block_no = index % sources * 4 + index // sources
    cos_first, sin_first = turning(index[:, None] * block_no[None, :], inner)
    first = jnp.concatenate([cos_first, -sin_first], axis=0)
    twist = turning_pair(index[:, None] * index[None, :], length, 0)
    kept = index // 4 * 2 + index % 2
    imag_row = (index // 2 % 2 == 1)[:, None]
    cos_second, sin_second = turning(kept[:, None] * index[None, :], LANES)
    scale = 1.0 / math.sqrt(length) / 16.0 / 4.0
    from_re = jnp.where(imag_row, -sin_second, cos_second) * scale
    from_im = jnp.where(imag_row, cos_second, sin_second) * scale
    return first, twist, jnp.concatenate([from_re, from_im], axis=1)


def transform_kernel(blocks_ref, first_ref, twist_ref, second_ref, out_ref, tall):
    channels = out_ref.shape[0] // LANES
    held = blocks_ref.shape[0]
    for r in range(blocks_ref.shape[1] // LANES):
        tall[r * held : (r + 1) * held, :] = blocks_ref[:, r * LANES : (r + 1) * LANES]
    first = jnp.concatenate(split_bf16(first_ref[...]), axis=1)
    second_high, second_low = split_bf16(second_ref[...])
    second = jnp.concatenate([second_high, second_low], axis=0)
    across = (((1,), (1,)), ((), ()))
    for pair in range(channels // 2):
        mine = (2 * pair, 2 * pair + 1)
        columns = [tall[pl.ds(c, LANES, stride=channels), :] for c in mine]
        part = products(first, *windows(jnp.concatenate(columns, axis=1)))
        rows = []
        for j in range(2):
            lanes = slice(j * LANES, (j + 1) * LANES)
            turned = rotate(part[:LANES, lanes], part[LANES:, lanes], twist_ref[0], twist_ref[1])
            rows.append(jnp.concatenate(turned, axis=1))
        high, low = split_bf16(jnp.concatenate(rows, axis=0))
        got = lax.dot_general(second, high, across, preferred_element_type=f32)
        got = (
            got[:LANES]
            + got[LANES:]
            + lax.dot_general(second_high, low, across, preferred_element_type=f32)
        )
        for j, c in enumerate(mine):
            out_ref[pl.ds(c, LANES, stride=channels), :] = got[:, j * LANES : (j + 1) * LANES]


def delay_turns(channel_delay, first_bin, length):
    per_sub = channel_delay.shape[0] // 2
    both = jnp.concatenate([channel_delay[:per_sub], channel_delay[per_sub:]], axis=1)
    halves = [2 * first_bin + GROUP - 1, 2 * GROUP, 1]
    count = both[None] * jnp.stack([jnp.int32(h) for h in halves])[:, None, None]
    return turning_pair(count, 2 * length, 1)


def add_angles(a, b):
    return (a[0] * b[0] - a[1] * b[1], a[1] * b[0] + a[0] * b[1])


def sub_kernel(
    quarters, spec_ref, tab_ref, tw_ref, out_ref, parts, centre, wide, offset, spread
):
    half = LANES // 2
    per_sub = centre.shape[2]
    sources = spec_ref.shape[0] // 2
    rows = spec_ref.shape[2]
    left = lax.broadcasted_iota(jnp.int32, (rows, LANES), 1) < half

    def arrange(g, carry):
        at = pl.ds(pl.multiple_of(rows * g, rows), rows)
        for x in range(2):
            to = pl.ds(pl.multiple_of(per_sub * x + rows * g, rows), rows)
            for slot, q in enumerate(quarters):
                first = spec_ref[g, 2 * x + q // 2]
                second = spec_ref[sources + g, 2 * x + q // 2]
                if q % 2 == 0:
                    pair = jnp.where(left, first, pltpu.roll(second, half, 1))
                else:
                    pair = jnp.where(left, pltpu.roll(first, half, 1), second)
                high, low = split_bf16(pair)
                parts[slot, to, 0:LANES] = high
                parts[slot, to, LANES:] = low
        first, step, unit = ((tab_ref[i, 0, at, :], tab_ref[i, 1, at, :]) for i in range(3))
        bin_turn = add_angles(unit, unit)
        for b in range(GROUP // 2):
            offset[b, 0, at, :], offset[b, 1, at, :] = unit
            unit = add_angles(unit, bin_turn)
        for _ in range(3):
            step = add_angles(step, step)
        for q in range(4):
            if q in quarters:
                slot = quarters.index(q)
                centre[slot, 0, at, :], centre[slot, 1, at, :] = first
            first = add_angles(first, step)
        return carry

    lax.fori_loop(0, sources, arrange, 0, unroll=2)
    passes = half // (2 * GROUP)
    source = lax.broadcasted_iota(jnp.int32, (LANES, 2 * LANES), 0)
    target = lax.broadcasted_iota(jnp.int32, (LANES, 2 * LANES), 1)
    apart = source - target // LANES - target % LANES // half * half

    def one_hots(n, carry):
        spread[n] = jnp.where(apart == 2 * n, 1.0, 0.0).astype(bf16)
        return carry

    lax.fori_loop(0, spread.shape[0], one_hots, 0)

    def bins(step, carry):
        slot = step // passes
        for n in range(GROUP):
            one_hot = spread[step % passes * GROUP + n]
            one_hot = jnp.concatenate([one_hot, one_hot], axis=0)
            for r in range(2):
                at = slice(r * per_sub, (r + 1) * per_sub)
                wide[n, at, :] = jnp.dot(
                    parts[slot, at, :],
                    one_hot,
                    preferred_element_type=f32,
                )

        def channels(g, sums):
            re = list(sums[: 2 * GROUP])
            im = list(sums[2 * GROUP :])
            at = pl.ds(pl.multiple_of(8 * g, 8), 8)
            at_im = pl.ds(pl.multiple_of(per_sub + 8 * g, 8), 8)
            advance = (tab_ref[1, 0, at, :], tab_ref[1, 1, at, :])
            mids = [(centre[slot, 0, at, :], centre[slot, 1, at, :])]
            mids.append(add_angles(mids[0], advance))
            for b in range(GROUP // 2):
                off_cos = offset[b, 0, at, :]
                off_sin = offset[b, 1, at, :]
                for h, (mid_cos, mid_sin) in enumerate(mids):
                    cc, ss = mid_cos * off_cos, mid_sin * off_sin
                    sc, cs = mid_sin * off_cos, mid_cos * off_sin
                    for j, cosine, sine in (
                        (h * GROUP + GROUP // 2 + b, cc - ss, sc + cs),
                        (h * GROUP + GROUP // 2 - 1 - b, cc + ss, sc - cs),
                    ):
                        lanes = slice(j % 2 * LANES, j % 2 * LANES + LANES)
                        real = wide[j // 2, at, lanes]
                        imag = wide[j // 2, at_im, lanes]
                        re[j] = re[j] + (real * cosine + imag * sine)
                        im[j] = im[j] + (imag * cosine - real * sine)
            centre[slot, 0, at, :], centre[slot, 1, at, :] = add_angles(mids[1], advance)
            return tuple(re) + tuple(im)

        zero = jnp.zeros((8, LANES), f32)
        sums = lax.fori_loop(0, per_sub // 8, channels, (zero,) * (4 * GROUP), unroll=per_sub // 8)
        at = pl.ds(pl.multiple_of(step * 2 * GROUP, 2 * GROUP), 2 * GROUP)
        re, im = (
            jnp.concatenate(
                [
                    jnp.sum(v, axis=0, keepdims=True)
                    for v in sums[x * 2 * GROUP : (x + 1) * 2 * GROUP]
                ],
                axis=0,
            )
            for x in range(2)
        )
        lower = lax.broadcasted_iota(jnp.int32, re.shape, 1) < half
        re_turn = pltpu.roll(re, half, 1)
        im_turn = pltpu.roll(im, half, 1)
        up_re, up_im = rotate(
            jnp.where(lower, re_turn, re),
            jnp.where(lower, im_turn, im),
            tw_ref[0, at, :],
            tw_ref[1, at, :],
        )
        out_ref[0, at, :] = jnp.where(lower, re, re_turn) + up_re
        out_ref[1, at, :] = jnp.where(lower, im, im_turn) + up_im
        return carry

    lax.fori_loop(0, out_ref.shape[1] // (2 * GROUP), bins, 0)


def toeplitz_kernel(profile_ref, band_ref):
    rows = 2 * REACH

    def body(a, carry):
        row = profile_ref[pl.ds(a, 1), :]
        wide = jnp.broadcast_to(row, (rows, row.shape[1]))
        high, low = split_bf16(pltpu.roll(wide, 0, 1, stride=1, stride_axis=0))
        at = pl.ds(pl.multiple_of(a * rows, rows), rows)
        band_ref[at, :LANES] = high
        band_ref[at, LANES:] = low
        return carry

    lax.fori_loop(0, profile_ref.shape[0], body, 0, unroll=4)


def windows(value):
    high, low = split_bf16(value)
    return jnp.concatenate([high, high], axis=0), jnp.concatenate([low, low], axis=0)


def products(band, high, low):
    return jnp.dot(band, high, preferred_element_type=f32) + jnp.dot(
        band, low, preferred_element_type=f32
    )


def power(value):
    re, im = value[:, :LANES], value[:, LANES:]
    return re * re + im * im


def inner_kernel(outer_ref, mid_ref, band_ref, out_ref):
    near = 2 * REACH
    columns = [
        jnp.concatenate([outer_ref[x, :near], mid_ref[x], outer_ref[x, near:]], axis=0)
        for x in range(2)
    ]
    whole = jnp.concatenate(columns, axis=1)
    per = 4
    for i in range(out_ref.shape[0] // near):
        high, low = windows(whole[i * near : i * near + LANES])
        best = jnp.zeros((near, LANES), f32)
        for step in range(band_ref.shape[0] // (per * near)):
            at = slice(step * per * near, (step + 1) * per * near)
            got = products(band_ref[at, :], high, low)
            for j in range(per):
                best = jnp.maximum(best, power(got[j * near : (j + 1) * near]))
        out_ref[i * near : (i + 1) * near, :] = best


def edge_kernel(left_ref, outer_ref, right_ref, inner_ref, band_ref, out_ref):
    near = 2 * REACH
    pad = jnp.zeros((LANES - 3 * REACH, LANES), f32)
    columns = [
        jnp.concatenate([left_ref[x], outer_ref[x, :near], pad], axis=0) for x in range(2)
    ] + [jnp.concatenate([outer_ref[x, near:], right_ref[x], pad], axis=0) for x in range(2)]
    high, low = windows(jnp.concatenate(columns, axis=1))
    per = 8
    best = [jnp.zeros((REACH, LANES), f32)] * 2
    for step in range(band_ref.shape[0] // (per * near)):
        first = step * per * near
        band = jnp.concatenate(
            [band_ref[first + i * near : first + i * near + REACH, :] for i in range(per)], axis=0
        )
        got = products(band, high, low)
        for i in range(per):
            mine = got[i * REACH : (i + 1) * REACH]
            for side in range(2):
                lanes = slice(side * 2 * LANES, (side + 1) * 2 * LANES)
                best[side] = jnp.maximum(best[side], power(mine[:, lanes]))
    out_ref[...] = jnp.concatenate([best[0], inner_ref[...], best[1]], axis=0).T


def per_device(samples, channel_delay, merge_slope, tap_offset, tap_weight):
    freq_count = lax.axis_size("freq")
    band_count = lax.axis_size("band")
    band_pos = lax.axis_index("band")
    freq_pos = lax.axis_index("freq")
    chan_dev, samp_dev = samples.shape
    length = samp_dev * freq_count
    bins_dev = length // 2 // freq_count
    delays_sub = channel_delay.shape[1]
    block = 2 * delays_sub
    vmem = pl.BlockSpec(memory_space=pltpu.VMEM)

    first_bin = freq_pos * bins_dev
    tabs = delay_turns(channel_delay, first_bin, length)
    sections = band_count.bit_length()
    shifts = []
    for s in range(sections):
        size = 1 << s
        slope = pick_entry(merge_slope, band_pos // size * (2 * size) + size - 1)
        out_index = band_pos % size * block + lax.iota(jnp.int32, block)
        shifts.append(out_index * slope // 16 % length)
    shifts = jnp.stack(shifts)
    chunks = ((0, 3), (1, 2))
    quarter = bins_dev // 4
    within = lax.iota(jnp.int32, quarter)
    turns = []
    for pair in chunks:
        bins_index = jnp.concatenate([first_bin + q * quarter + within for q in pair])
        count = shifts[:, None, :] * bins_index[None, :, None]
        turns.append(
            (
                turning_pair(count[0], length, 0),
                turning_pair(count[1:], length, 1),
            )
        )
    matches = tap_offset[:, :, None] + REACH == lax.iota(jnp.int32, LANES)[None, None, :]
    profile = jnp.sum(jnp.where(matches, tap_weight[:, :, None], 0.0), axis=1)
    templates = profile.shape[0]
    band = pl.pallas_call(
        toeplitz_kernel,
        out_shape=jax.ShapeDtypeStruct((templates * 2 * REACH, 2 * LANES), bf16),
        in_specs=[vmem],
        out_specs=vmem,
        compiler_params=pltpu.CompilerParams(vmem_limit_bytes=FILTER_VMEM),
        name="toeplitz",
    )(profile)

    tables = transform_tables(length)
    blocks = samples.reshape(freq_count, chan_dev // freq_count, samp_dev)
    blocks = lax.all_to_all(blocks, "freq", split_axis=0, concat_axis=0, tiled=True)
    spec = pl.pallas_call(
        transform_kernel,
        out_shape=jax.ShapeDtypeStruct((chan_dev // freq_count * LANES, LANES), f32),
        in_specs=[vmem] * 4,
        out_specs=vmem,
        scratch_shapes=[pltpu.VMEM((chan_dev // freq_count * LANES, LANES), f32)],
        compiler_params=pltpu.CompilerParams(vmem_limit_bytes=FILTER_VMEM),
        name="transform",
    )(blocks.reshape(chan_dev, samp_dev), *tables)
    spec = spec.reshape(freq_count, chan_dev * 4 // freq_count, LANES)
    spec = lax.all_to_all(spec, "freq", split_axis=0, concat_axis=0, tiled=True)
    spec = spec.reshape(freq_count, 4, chan_dev // freq_count, LANES)
    spec, turns, tabs, band = lax.optimization_barrier((spec, turns, tabs, band))

    current = []
    for pair, turn in zip(chunks, turns):
        current.append(
            pl.pallas_call(
                functools.partial(sub_kernel, pair),
                out_shape=jax.ShapeDtypeStruct((2, bins_dev // 2, block), f32),
                in_specs=[vmem] * 3,
                out_specs=vmem,
                scratch_shapes=[
                    pltpu.VMEM((2, chan_dev, 2 * LANES), bf16),
                    pltpu.VMEM((2, 2, chan_dev // 2, LANES), f32),
                    pltpu.VMEM((GROUP, chan_dev, 2 * LANES), f32),
                    pltpu.VMEM((GROUP // 2, 2, chan_dev // 2, LANES), f32),
                    pltpu.VMEM((LANES // 4, LANES, 2 * LANES), bf16),
                ],
                cost_estimate=pl.CostEstimate(
                    flops=10**10, bytes_accessed=2**23, transcendentals=0
                ),
                compiler_params=pltpu.CompilerParams(vmem_limit_bytes=SUB_VMEM),
                name="subband",
            )(spec, tabs, turn[0])
        )

    for s in range(1, sections):
        half = 1 << (s - 1)
        for i in range(len(chunks)):
            mine = current[i]
            partner = lax.ppermute(mine, "band", [(j, j ^ half) for j in range(band_count)])
            upper_side = band_pos % (2 * half) >= half
            lower = jnp.where(upper_side, partner, mine)
            upper = jnp.where(upper_side, mine, partner)
            turn = turns[i][1][s - 1]
            up_re, up_im = rotate(upper[0], upper[1], turn[0], turn[1])
            current[i] = jnp.stack([lower[0] + up_re, lower[1] + up_im])

    outer, middle = current
    ends = freq_count - 1
    from_left = lax.ppermute(
        outer[:, bins_dev // 2 - REACH :], "freq", [(i, i + 1) for i in range(ends)]
    )
    from_right = lax.ppermute(outer[:, :REACH], "freq", [(i + 1, i) for i in range(ends)])
    inner = pl.pallas_call(
        inner_kernel,
        out_shape=jax.ShapeDtypeStruct((bins_dev - 2 * REACH, block), f32),
        in_specs=[vmem] * 3,
        out_specs=vmem,
        cost_estimate=pl.CostEstimate(flops=2 * 10**9, bytes_accessed=2**21, transcendentals=0),
        compiler_params=pltpu.CompilerParams(vmem_limit_bytes=FILTER_VMEM),
        name="inner_bins",
    )(outer, middle, band)
    return pl.pallas_call(
        edge_kernel,
        out_shape=jax.ShapeDtypeStruct((block, bins_dev), f32),
        in_specs=[vmem] * 5,
        out_specs=vmem,
        compiler_params=pltpu.CompilerParams(vmem_limit_bytes=FILTER_VMEM),
        name="edge_bins",
    )(from_left, outer, from_right, inner, band)


def solution(mesh):
    placed = (P("band", "freq"), P("band", None), P(), P(), P())
    return jax.shard_map(
        per_device, mesh=mesh, in_specs=placed, out_specs=P("band", "freq"), check_vma=False
    )
```

```python
import functools
import math

import jax
import jax.numpy as jnp
from jax import lax
from jax.experimental import pallas as pl
from jax.experimental.pallas import tpu as pltpu
from jax.sharding import PartitionSpec as P

REACH = 32
LANES = 128
GROUP = 8
SUB_VMEM = 14 * 2**20
FILTER_VMEM = 8 * 2**20

two_pi = 2.0 * math.pi
f32 = jnp.float32
bf16 = jnp.bfloat16


def turning(count, modulus):
    angle = (count % modulus).astype(f32) * (two_pi / modulus)
    return (jnp.cos(angle), jnp.sin(angle))


def turning_pair(count, modulus, axis):
    quarter_back = jnp.array([0, modulus // 4 * 3], jnp.int32)
    offset = quarter_back.reshape([2 if i == axis else 1 for i in range(count.ndim + 1)])
    return turning(jnp.expand_dims(count, axis) + offset, modulus)[0]


def rotate(real, imag, cosine, sine_part):
    return (real * cosine + imag * sine_part, imag * cosine - real * sine_part)


def pick_entry(table, index):
    return jnp.sum(jnp.where(lax.iota(jnp.int32, table.shape[0]) == index, table, 0))


def split_bf16(value):
    high = value.astype(bf16)
    return high, (value - high.astype(f32)).astype(bf16)


def transform_tables(length):
    inner = length // LANES
    index = lax.iota(jnp.int32, LANES)
    sources = LANES // 4
    block_no = index % sources * 4 + index // sources
    cos_first, sin_first = turning(index[:, None] * block_no[None, :], inner)
    first = jnp.concatenate([cos_first, -sin_first], axis=0)
    twist = turning_pair(index[:, None] * index[None, :], length, 0)
    kept = index // 4 * 2 + index % 2
    imag_row = (index // 2 % 2 == 1)[:, None]
    cos_second, sin_second = turning(kept[:, None] * index[None, :], LANES)
    scale = 1.0 / math.sqrt(length) / 16.0 / 4.0
    from_re = jnp.where(imag_row, -sin_second, cos_second) * scale
    from_im = jnp.where(imag_row, cos_second, sin_second) * scale
    return first, twist, jnp.concatenate([from_re, from_im], axis=1)


def transform_kernel(blocks_ref, first_ref, twist_ref, second_ref, out_ref, tall):
    channels = out_ref.shape[0] // LANES
    held = blocks_ref.shape[0]
    for r in range(blocks_ref.shape[1] // LANES):
        tall[r * held : (r + 1) * held, :] = blocks_ref[:, r * LANES : (r + 1) * LANES]
    first = jnp.concatenate(split_bf16(first_ref[...]), axis=1)
    second_high, second_low = split_bf16(second_ref[...])
    second = jnp.concatenate([second_high, second_low], axis=0)
    across = (((1,), (1,)), ((), ()))
    for pair in range(channels // 2):
        mine = (2 * pair, 2 * pair + 1)
        columns = [tall[pl.ds(c, LANES, stride=channels), :] for c in mine]
        part = products(first, *windows(jnp.concatenate(columns, axis=1)))
        rows = []
        for j in range(2):
            lanes = slice(j * LANES, (j + 1) * LANES)
            turned = rotate(part[:LANES, lanes], part[LANES:, lanes], twist_ref[0], twist_ref[1])
            rows.append(jnp.concatenate(turned, axis=1))
        high, low = split_bf16(jnp.concatenate(rows, axis=0))
        got = lax.dot_general(second, high, across, preferred_element_type=f32)
        got = (
            got[:LANES]
            + got[LANES:]
            + lax.dot_general(second_high, low, across, preferred_element_type=f32)
        )
        for j, c in enumerate(mine):
            out_ref[pl.ds(c, LANES, stride=channels), :] = got[:, j * LANES : (j + 1) * LANES]


def delay_turns(channel_delay, first_bin, length):
    per_sub = channel_delay.shape[0] // 2
    both = jnp.concatenate([channel_delay[:per_sub], channel_delay[per_sub:]], axis=1)
    halves = [2 * first_bin + GROUP - 1, 2 * GROUP, 1]
    count = both[None] * jnp.stack([jnp.int32(h) for h in halves])[:, None, None]
    return turning_pair(count, 2 * length, 1)


def add_angles(a, b):
    return (a[0] * b[0] - a[1] * b[1], a[1] * b[0] + a[0] * b[1])


def sub_kernel(
    quarters, spec_ref, tab_ref, tw_ref, out_ref, parts, centre, wide, offset, spread
):
    half = LANES // 2
    per_sub = centre.shape[2]
    sources = spec_ref.shape[0] // 2
    rows = spec_ref.shape[2]
    left = lax.broadcasted_iota(jnp.int32, (rows, LANES), 1) < half

    def arrange(g, carry):
        at = pl.ds(pl.multiple_of(rows * g, rows), rows)
        for x in range(2):
            to = pl.ds(pl.multiple_of(per_sub * x + rows * g, rows), rows)
            for slot, q in enumerate(quarters):
                first = spec_ref[g, 2 * x + q // 2]
                second = spec_ref[sources + g, 2 * x + q // 2]
                if q % 2 == 0:
                    pair = jnp.where(left, first, pltpu.roll(second, half, 1))
                else:
                    pair = jnp.where(left, pltpu.roll(first, half, 1), second)
                high, low = split_bf16(pair)
                parts[slot, to, 0:LANES] = high
                parts[slot, to, LANES:] = low
        first, step, unit = ((tab_ref[i, 0, at, :], tab_ref[i, 1, at, :]) for i in range(3))
        bin_turn = add_angles(unit, unit)
        for b in range(2):
            offset[b, 0, at, :], offset[b, 1, at, :] = unit
            unit = add_angles(unit, bin_turn)
        for _ in range(3):
            step = add_angles(step, step)
        for q in range(4):
            if q in quarters:
                slot = quarters.index(q)
                centre[slot, 0, at, :], centre[slot, 1, at, :] = first
            first = add_angles(first, step)
        return carry

    lax.fori_loop(0, sources, arrange, 0, unroll=2)
    passes = half // (2 * GROUP)
    source = lax.broadcasted_iota(jnp.int32, (LANES, 2 * LANES), 0)
    target = lax.broadcasted_iota(jnp.int32, (LANES, 2 * LANES), 1)
    apart = source - target // LANES - target % LANES // half * half

    def one_hots(n, carry):
        spread[n] = jnp.where(apart == 2 * n, 1.0, 0.0).astype(bf16)
        return carry

    lax.fori_loop(0, spread.shape[0], one_hots, 0)

    def bins(step, carry):
        slot = step // passes
        for n in range(GROUP):
            one_hot = spread[step % passes * GROUP + n]
            one_hot = jnp.concatenate([one_hot, one_hot], axis=0)
            for r in range(2):
                at = slice(r * per_sub, (r + 1) * per_sub)
                wide[n, at, :] = jnp.dot(
                    parts[slot, at, :],
                    one_hot,
                    preferred_element_type=f32,
                )

        def channels(g, sums):
            re = list(sums[: 2 * GROUP])
            im = list(sums[2 * GROUP :])
            at = pl.ds(pl.multiple_of(8 * g, 8), 8)
            at_im = pl.ds(pl.multiple_of(per_sub + 8 * g, 8), 8)
            advance = (tab_ref[1, 0, at, :], tab_ref[1, 1, at, :])
            mids = [(centre[slot, 0, at, :], centre[slot, 1, at, :])]
            mids.append(add_angles(mids[0], advance))
            offs = [(offset[b, 0, at, :], offset[b, 1, at, :]) for b in range(2)]
            bin_turn = add_angles(offs[1], (offs[0][0], -offs[0][1]))
            for b in range(2, GROUP // 2):
                offs.append(add_angles(offs[-1], bin_turn))
            for b, (off_cos, off_sin) in enumerate(offs):
                for h, (mid_cos, mid_sin) in enumerate(mids):
                    cc, ss = mid_cos * off_cos, mid_sin * off_sin
                    sc, cs = mid_sin * off_cos, mid_cos * off_sin
                    for j, cosine, sine in (
                        (h * GROUP + GROUP // 2 + b, cc - ss, sc + cs),
                        (h * GROUP + GROUP // 2 - 1 - b, cc + ss, sc - cs),
                    ):
                        lanes = slice(j % 2 * LANES, j % 2 * LANES + LANES)
                        real = wide[j // 2, at, lanes]
                        imag = wide[j // 2, at_im, lanes]
                        re[j] = re[j] + (real * cosine + imag * sine)
                        im[j] = im[j] + (imag * cosine - real * sine)
            centre[slot, 0, at, :], centre[slot, 1, at, :] = add_angles(mids[1], advance)
            return tuple(re) + tuple(im)

        zero = jnp.zeros((8, LANES), f32)
        sums = lax.fori_loop(0, per_sub // 8, channels, (zero,) * (4 * GROUP), unroll=per_sub // 8)
        at = pl.ds(pl.multiple_of(step * 2 * GROUP, 2 * GROUP), 2 * GROUP)
        re, im = (
            jnp.concatenate(
                [
                    jnp.sum(v, axis=0, keepdims=True)
                    for v in sums[x * 2 * GROUP : (x + 1) * 2 * GROUP]
                ],
                axis=0,
            )
            for x in range(2)
        )
        lower = lax.broadcasted_iota(jnp.int32, re.shape, 1) < half
        re_turn = pltpu.roll(re, half, 1)
        im_turn = pltpu.roll(im, half, 1)
        up_re, up_im = rotate(
            jnp.where(lower, re_turn, re),
            jnp.where(lower, im_turn, im),
            tw_ref[0, at, :],
            tw_ref[1, at, :],
        )
        out_ref[0, at, :] = jnp.where(lower, re, re_turn) + up_re
        out_ref[1, at, :] = jnp.where(lower, im, im_turn) + up_im
        return carry

    lax.fori_loop(0, out_ref.shape[1] // (2 * GROUP), bins, 0)


def toeplitz_kernel(profile_ref, band_ref):
    rows = 2 * REACH

    def body(a, carry):
        row = profile_ref[pl.ds(a, 1), :]
        wide = jnp.broadcast_to(row, (rows, row.shape[1]))
        high, low = split_bf16(pltpu.roll(wide, 0, 1, stride=1, stride_axis=0))
        at = pl.ds(pl.multiple_of(a * rows, rows), rows)
        band_ref[at, :LANES] = high
        band_ref[at, LANES:] = low
        return carry

    lax.fori_loop(0, profile_ref.shape[0], body, 0, unroll=4)


def windows(value):
    high, low = split_bf16(value)
    return jnp.concatenate([high, high], axis=0), jnp.concatenate([low, low], axis=0)


def products(band, high, low):
    return jnp.dot(band, high, preferred_element_type=f32) + jnp.dot(
        band, low, preferred_element_type=f32
    )


def power(value):
    re, im = value[:, :LANES], value[:, LANES:]
    return re * re + im * im


def inner_kernel(outer_ref, mid_ref, band_ref, out_ref):
    near = 2 * REACH
    columns = [
        jnp.concatenate([outer_ref[x, :near], mid_ref[x], outer_ref[x, near:]], axis=0)
        for x in range(2)
    ]
    whole = jnp.concatenate(columns, axis=1)
    per = 4
    for i in range(out_ref.shape[0] // near):
        high, low = windows(whole[i * near : i * near + LANES])
        best = jnp.zeros((near, LANES), f32)
        for step in range(band_ref.shape[0] // (per * near)):
            at = slice(step * per * near, (step + 1) * per * near)
            got = products(band_ref[at, :], high, low)
            for j in range(per):
                best = jnp.maximum(best, power(got[j * near : (j + 1) * near]))
        out_ref[i * near : (i + 1) * near, :] = best


def edge_kernel(left_ref, outer_ref, right_ref, inner_ref, band_ref, out_ref):
    near = 2 * REACH
    pad = jnp.zeros((LANES - 3 * REACH, LANES), f32)
    columns = [
        jnp.concatenate([left_ref[x], outer_ref[x, :near], pad], axis=0) for x in range(2)
    ] + [jnp.concatenate([outer_ref[x, near:], right_ref[x], pad], axis=0) for x in range(2)]
    high, low = windows(jnp.concatenate(columns, axis=1))
    per = 8
    best = [jnp.zeros((REACH, LANES), f32)] * 2
    for step in range(band_ref.shape[0] // (per * near)):
        first = step * per * near
        band = jnp.concatenate(
            [band_ref[first + i * near : first + i * near + REACH, :] for i in range(per)], axis=0
        )
        got = products(band, high, low)
        for i in range(per):
            mine = got[i * REACH : (i + 1) * REACH]
            for side in range(2):
                lanes = slice(side * 2 * LANES, (side + 1) * 2 * LANES)
                best[side] = jnp.maximum(best[side], power(mine[:, lanes]))
    out_ref[...] = jnp.concatenate([best[0], inner_ref[...], best[1]], axis=0).T


def per_device(samples, channel_delay, merge_slope, tap_offset, tap_weight):
    freq_count = lax.axis_size("freq")
    band_count = lax.axis_size("band")
    band_pos = lax.axis_index("band")
    freq_pos = lax.axis_index("freq")
    chan_dev, samp_dev = samples.shape
    length = samp_dev * freq_count
    bins_dev = length // 2 // freq_count
    delays_sub = channel_delay.shape[1]
    block = 2 * delays_sub
    vmem = pl.BlockSpec(memory_space=pltpu.VMEM)

    first_bin = freq_pos * bins_dev
    tabs = delay_turns(channel_delay, first_bin, length)
    sections = band_count.bit_length()
    shifts = []
    for s in range(sections):
        size = 1 << s
        slope = pick_entry(merge_slope, band_pos // size * (2 * size) + size - 1)
        out_index = band_pos % size * block + lax.iota(jnp.int32, block)
        shifts.append(out_index * slope // 16 % length)
    shifts = jnp.stack(shifts)
    chunks = ((0, 3), (1, 2))
    quarter = bins_dev // 4
    within = lax.iota(jnp.int32, quarter)
    turns = []
    for pair in chunks:
        bins_index = jnp.concatenate([first_bin + q * quarter + within for q in pair])
        count = shifts[:, None, :] * bins_index[None, :, None]
        turns.append(
            (
                turning_pair(count[0], length, 0),
                turning_pair(count[1:], length, 1),
            )
        )
    matches = tap_offset[:, :, None] + REACH == lax.iota(jnp.int32, LANES)[None, None, :]
    profile = jnp.sum(jnp.where(matches, tap_weight[:, :, None], 0.0), axis=1)
    templates = profile.shape[0]
    band = pl.pallas_call(
        toeplitz_kernel,
        out_shape=jax.ShapeDtypeStruct((templates * 2 * REACH, 2 * LANES), bf16),
        in_specs=[vmem],
        out_specs=vmem,
        compiler_params=pltpu.CompilerParams(vmem_limit_bytes=FILTER_VMEM),
        name="toeplitz",
    )(profile)

    tables = transform_tables(length)
    blocks = samples.reshape(freq_count, chan_dev // freq_count, samp_dev)
    blocks = lax.all_to_all(blocks, "freq", split_axis=0, concat_axis=0, tiled=True)
    spec = pl.pallas_call(
        transform_kernel,
        out_shape=jax.ShapeDtypeStruct((chan_dev // freq_count * LANES, LANES), f32),
        in_specs=[vmem] * 4,
        out_specs=vmem,
        scratch_shapes=[pltpu.VMEM((chan_dev // freq_count * LANES, LANES), f32)],
        compiler_params=pltpu.CompilerParams(vmem_limit_bytes=FILTER_VMEM),
        name="transform",
    )(blocks.reshape(chan_dev, samp_dev), *tables)
    spec = spec.reshape(freq_count, chan_dev * 4 // freq_count, LANES)
    spec = lax.all_to_all(spec, "freq", split_axis=0, concat_axis=0, tiled=True)
    spec = spec.reshape(freq_count, 4, chan_dev // freq_count, LANES)
    spec, turns, tabs, band = lax.optimization_barrier((spec, turns, tabs, band))

    current = []
    for pair, turn in zip(chunks, turns):
        current.append(
            pl.pallas_call(
                functools.partial(sub_kernel, pair),
                out_shape=jax.ShapeDtypeStruct((2, bins_dev // 2, block), f32),
                in_specs=[vmem] * 3,
                out_specs=vmem,
                scratch_shapes=[
                    pltpu.VMEM((2, chan_dev, 2 * LANES), bf16),
                    pltpu.VMEM((2, 2, chan_dev // 2, LANES), f32),
                    pltpu.VMEM((GROUP, chan_dev, 2 * LANES), f32),
                    pltpu.VMEM((2, 2, chan_dev // 2, LANES), f32),
                    pltpu.VMEM((LANES // 4, LANES, 2 * LANES), bf16),
                ],
                cost_estimate=pl.CostEstimate(
                    flops=10**10, bytes_accessed=2**23, transcendentals=0
                ),
                compiler_params=pltpu.CompilerParams(vmem_limit_bytes=SUB_VMEM),
                name="subband",
            )(spec, tabs, turn[0])
        )

    for s in range(1, sections):
        half = 1 << (s - 1)
        for i in range(len(chunks)):
            mine = current[i]
            partner = lax.ppermute(mine, "band", [(j, j ^ half) for j in range(band_count)])
            upper_side = band_pos % (2 * half) >= half
            lower = jnp.where(upper_side, partner, mine)
            upper = jnp.where(upper_side, mine, partner)
            turn = turns[i][1][s - 1]
            up_re, up_im = rotate(upper[0], upper[1], turn[0], turn[1])
            current[i] = jnp.stack([lower[0] + up_re, lower[1] + up_im])

    outer, middle = current
    ends = freq_count - 1
    from_left = lax.ppermute(
        outer[:, bins_dev // 2 - REACH :], "freq", [(i, i + 1) for i in range(ends)]
    )
    from_right = lax.ppermute(outer[:, :REACH], "freq", [(i + 1, i) for i in range(ends)])
    inner = pl.pallas_call(
        inner_kernel,
        out_shape=jax.ShapeDtypeStruct((bins_dev - 2 * REACH, block), f32),
        in_specs=[vmem] * 3,
        out_specs=vmem,
        cost_estimate=pl.CostEstimate(flops=2 * 10**9, bytes_accessed=2**21, transcendentals=0),
        compiler_params=pltpu.CompilerParams(vmem_limit_bytes=FILTER_VMEM),
        name="inner_bins",
    )(outer, middle, band)
    return pl.pallas_call(
        edge_kernel,
        out_shape=jax.ShapeDtypeStruct((block, bins_dev), f32),
        in_specs=[vmem] * 5,
        out_specs=vmem,
        compiler_params=pltpu.CompilerParams(vmem_limit_bytes=FILTER_VMEM),
        name="edge_bins",
    )(from_left, outer, from_right, inner, band)


def solution(mesh):
    placed = (P("band", "freq"), P("band", None), P(), P(), P())
    return jax.shard_map(
        per_device, mesh=mesh, in_specs=placed, out_specs=P("band", "freq"), check_vma=False
    )
```
